128 devices in a mesh: section: 8 (over z_hi, x), tp: 16 (over y, z_lo, core).
Axes of the slice: x: 4, y: 4, z: 4 (z_hi: 2, z_lo: 2; z = z_hi * 2 + z_lo), core: 2. Of those that a mesh axis runs over, the one named last changes fastest.
Arguments:
- hidden_in: bfloat16 [2, 128, 8192], P(None, None, 'tp'), may hold values from -11.25 to 11.25
- norm_gain: float32 [8, 8192], P('section'), may hold values from 0.5 to 2
- w_query: bfloat16 [8, 8192, 8192], P('section', None, 'tp'), may hold values from -0.375 to 2.125
- w_key_value: bfloat16 [8, 8192, 2048], P('section', None, 'tp'), may hold values from -0.0625 to 0.0625
- w_out: bfloat16 [8, 8192, 8192], P('section', 'tp'), may hold values from -0.0625 to 0.0625
- cache: bfloat16 [8, 2, 16384, 256], P('section', None, 'tp'), may hold values from -6 to 6
- ctx_len: int32 [2], replicated, may hold values from 512 to 2048, as said below
- placement: int32 [8, 8, 2], P('section'), may hold values from 0 to 15, as said below
Outputs:
- layer_outputs: bfloat16 [8, 2, 128, 8192], P('section', None, None, 'tp')
- kv_store: bfloat16 [8, 32, 128, 256], P('section', 'tp')
The draws below stay inside these ranges and needn't reach their ends.
Inputs may be any that keep to these rules, and one draw needn't show every extreme that they name: `ctx_len`: one micro-batch has exactly 2048 cached tokens. `placement`: no holder receives more than 2 blocks of one layer, and in every layer some holder receives exactly 2.
All inputs are finite; a program needn't handle non-finite values.
Results may differ from the reference program's by a relative error of at most 0.028.
Values may be sent and summed in bfloat16 or wider, within the bound.
No kernel may reach another device: no remote copies, remote signals or barrier semaphores. Data moves between devices by JAX's collectives and lax.ppermute only.
A program may use at most 64 MiB of HBM per device.

```python
import math
import jax
import jax.numpy as jnp
from jax import lax

D = 8192
HEADS = 64
KVH = 8
HD = 128
SPAN = 128
MB = 2
SLOTS = 2
CTX = 2048
LAYERS = 8
TP_HEADS = 4
N_TP = 16


def draw_hidden_in(key, part):
    key = jax.random.fold_in(key, 3)
    noise_key, rough_key = jax.random.split(key, 2)
    noise = jnp.clip(jax.random.normal(noise_key, (MB, SPAN, D), jnp.float32), -4.0, 4.0)
    ramp = jnp.exp((jnp.arange(D, dtype=jnp.float32) / D - 0.5) * math.log(4.0))
    rough = jnp.exp(jax.random.uniform(rough_key, (D,), jnp.float32, math.log(0.7), math.log(1.4)))
    values = noise * (ramp * rough)[None, None, :]
    return values.astype(jnp.bfloat16)


def draw_w_query(key, part):
    key = jax.random.fold_in(key, 7)
    weight_key = jax.random.fold_in(key, 0)
    values = jnp.clip(jax.random.normal(weight_key, (LAYERS, D, HEADS * HD), jnp.float32), -3.0, 3.0) / math.sqrt(D)
    return values.astype(jnp.bfloat16)


def draw_cache(key, part):
    key = jax.random.fold_in(key, 13)
    values = jnp.clip(jax.random.normal(key, (LAYERS, MB, KVH, CTX, 2 * HD), jnp.float32), -6.0, 6.0)
    return values.reshape(LAYERS, MB, KVH * CTX, 2 * HD).astype(jnp.bfloat16)


def draw_ctx_len(key, part):
    key = jax.random.fold_in(key, 5)
    first_key, second_key = jax.random.split(key)
    lengths = jax.random.randint(first_key, (MB,), CTX // 4, CTX + 1)
    full = jax.random.randint(second_key, (), 0, MB)
    return jnp.where(jnp.arange(MB) == full, CTX, lengths).astype(jnp.int32)


def draw_placement(key, part):
    key = jax.random.fold_in(key, 11)
    entries = KVH * MB

    def one_layer(layer_key):
        first_key, second_key, third_key = jax.random.split(layer_key, 3)
        pool = jnp.arange(N_TP * SLOTS, dtype=jnp.int32)
        busiest = jax.random.randint(first_key, (), 0, N_TP)
        order = jax.random.permutation(second_key, N_TP * SLOTS).astype(jnp.int32)
        score = jnp.where(pool // SLOTS == busiest, -1 - pool, order)
        picked = jnp.argsort(score, stable=True)[:entries]
        holders = jax.random.permutation(third_key, picked // SLOTS)
        return holders.reshape(KVH, MB)
    return jax.vmap(one_layer)(jax.random.split(key, LAYERS)).astype(jnp.int32)


def block_scale(stream_key, dims, cuts, smallest, high):
    gain = 1.0
    for position, parts in cuts:
        draws = jax.random.uniform(jax.random.fold_in(jax.random.fold_in(stream_key, 6), position), (parts,), jnp.float32, smallest / len(cuts), high / len(cuts))
        gain = gain * jnp.repeat(jnp.exp(draws), dims[position] // parts).reshape((-1,) + (1,) * (len(dims) - 1 - position))
    return gain


def centred(rng, extent, scale, reach, cuts=(), kind=jnp.bfloat16):
    values = jax.random.normal(rng, extent, jnp.float32) * scale
    if len(cuts) > 0:
        values = block_scale(rng, extent, cuts, -0.22, 0.18) * values
    return jnp.clip(values, min=-reach, max=reach).astype(kind)


def setup_inputs(seed: int = 0) -> dict:
    arg_keys = jax.random.split(jax.random.key(seed), 9)
    hidden_in = draw_hidden_in(jax.random.fold_in(arg_keys[8], 71), 0)
    norm_gain = jnp.clip(jnp.exp(math.log(2.0) - 1.3862944 * jax.random.uniform(arg_keys[1], (LAYERS, D), jnp.float32) ** block_scale(arg_keys[1], (LAYERS, D), ((0, 8),), -0.2, 0.2)), 0.5, 2.0)
    w_query = draw_w_query(jax.random.fold_in(arg_keys[8], 71), 0)
    w_key_value = centred(arg_keys[3], (LAYERS, D, 2 * KVH * HD), D ** -0.5, 0.0625, ((0, 8), (2, 16)))
    w_out = centred(arg_keys[4], (LAYERS, HEADS * HD, D), (HEADS * HD) ** -0.5, 0.0625, ((0, 8), (1, 16)))
    cache = draw_cache(jax.random.fold_in(arg_keys[8], 71), 0)
    ctx_len = draw_ctx_len(jax.random.fold_in(arg_keys[8], 71), 0)
    placement = draw_placement(jax.random.fold_in(arg_keys[8], 71), 0)
    return dict(hidden_in=hidden_in, norm_gain=norm_gain, w_query=w_query, w_key_value=w_key_value, w_out=w_out, cache=cache, ctx_len=ctx_len, placement=placement)


def rotate(values, positions):
    half = values.shape[-1] // 2
    freqs = jnp.exp(jnp.arange(half, dtype=jnp.float32) * (-2.0 * math.log(500000.0) / values.shape[-1]))
    angles = positions.astype(jnp.float32)[:, None] * freqs[None, :]
    shape = (angles.shape[0],) + (1,) * (values.ndim - 2) + (half,)
    cosine = jnp.cos(angles).reshape(shape)
    sine = jnp.sin(angles).reshape(shape)
    first = values[..., :half]
    second = values[..., half:]
    return jnp.concatenate([first * cosine - second * sine, second * cosine + first * sine], axis=-1)

def reference(hidden_in, norm_gain, w_query, w_key_value, w_out, cache, ctx_len, placement):
    group = N_TP // KVH
    state = [hidden_in[m] for m in range(MB)]
    causal = jnp.arange(SPAN)[None, :] <= jnp.arange(SPAN)[:, None]
    layer_list = []
    store_list = []
    width = TP_HEADS * HD
    for layer in range(LAYERS):
        outs_layer = []
        fresh = []
        for micro in range(MB):
            wide = state[micro].astype(jnp.float32)
            normed = (wide * lax.rsqrt(lax.optimization_barrier(jnp.mean(wide * wide, axis=-1, keepdims=True)) + 1e-05) * norm_gain[layer]).astype(jnp.bfloat16)
            positions = ctx_len[micro] + jnp.arange(SPAN, dtype=jnp.int32)
            queries = jnp.dot(normed, w_query[layer], preferred_element_type=jnp.float32).reshape(SPAN, HEADS, HD)
            queries = rotate(queries, positions).astype(jnp.bfloat16)
            columns = jnp.dot(normed, w_key_value[layer], preferred_element_type=jnp.float32)
            columns = columns.reshape(SPAN, KVH, group, 2, HD // group)
            columns = jnp.transpose(columns, (0, 1, 3, 2, 4)).reshape(SPAN, KVH, 2, HD)
            keys = rotate(columns[:, :, 0], positions).astype(jnp.bfloat16)
            values = columns[:, :, 1].astype(jnp.bfloat16)
            context = cache[layer, micro].reshape(KVH, CTX, 2 * HD).astype(jnp.float32)
            grouped = queries.astype(jnp.float32).reshape(SPAN, KVH, HEADS // KVH, HD)
            cached_scores = jnp.einsum('qgjd,gkd->gjqk', grouped, context[..., :HD]) / math.sqrt(HD)
            live = jnp.arange(CTX) < ctx_len[micro]
            cached_scores = jnp.where(live[None, None, None, :], cached_scores, -1e+30)
            fresh_scores = jnp.einsum('qgjd,kgd->gjqk', grouped, keys.astype(jnp.float32)) / math.sqrt(HD)
            fresh_scores = jnp.where(causal[None, None], fresh_scores, -1e+30)
            top = jnp.maximum(lax.optimization_barrier(jnp.max(cached_scores, axis=-1)), lax.optimization_barrier(jnp.max(fresh_scores, axis=-1)))
            cached_weights = jnp.exp(cached_scores - top[..., None])
            fresh_weights = jnp.exp(fresh_scores - top[..., None])
            total = lax.optimization_barrier(jnp.sum(cached_weights, axis=-1)) + lax.optimization_barrier(jnp.sum(fresh_weights, axis=-1))
            cached_round = lax.optimization_barrier(cached_weights.astype(jnp.bfloat16)).astype(jnp.float32)
            fresh_round = lax.optimization_barrier(fresh_weights.astype(jnp.bfloat16)).astype(jnp.float32)
            mixed = jnp.einsum('gjqk,gkd->qgjd', cached_round, context[..., HD:])
            mixed = mixed + jnp.einsum('gjqk,kgd->qgjd', fresh_round, values.astype(jnp.float32))
            attended = (mixed / jnp.transpose(total, (2, 0, 1))[..., None]).reshape(SPAN, HEADS * HD).astype(jnp.bfloat16)
            summed = jnp.zeros((SPAN, D), jnp.float32)
            for piece_index in range(N_TP):
                term = jnp.dot(attended[:, piece_index * width:(piece_index + 1) * width], w_out[layer, piece_index * width:(piece_index + 1) * width], preferred_element_type=jnp.float32).astype(jnp.bfloat16)
                summed = summed + lax.optimization_barrier(term).astype(jnp.float32)
            updated = (wide + summed).astype(jnp.bfloat16)
            state[micro] = updated
            outs_layer.append(updated)
            fresh.append(jnp.concatenate([keys, values], axis=-1))
        layer_list.append(jnp.stack(outs_layer))
        blocks = jnp.transpose(jnp.stack(fresh), (2, 0, 1, 3)).reshape(KVH * MB, SPAN, 2 * HD)
        holders = placement[layer].reshape(-1).astype(jnp.int32)
        count = holders.shape[0]
        earlier = (holders[None, :] == holders[:, None]) & (jnp.arange(count)[None, :] < jnp.arange(count)[:, None])
        ranks = lax.optimization_barrier(jnp.sum(earlier.astype(jnp.int32), axis=-1)).astype(jnp.int32)
        store = jnp.zeros((N_TP * SLOTS, SPAN, 2 * HD), jnp.bfloat16).at[holders * SLOTS + ranks].set(blocks)
        store_list.append(store)
    return (jnp.stack(layer_list), jnp.stack(store_list))
```

```python
import functools
import math

import jax
import jax.numpy as jnp
from jax import lax
from jax.experimental import pallas as pl
from jax.experimental.pallas import tpu as pltpu
from jax.sharding import Mesh
from jax.sharding import PartitionSpec as P

HD = 128
SLOTS = 2
EPS = 1e-05
ROWS = 64
LIMIT = 16 * 2**20


def swap(x):
    return lax.ppermute(x, "core", [(0, 1), (1, 0)])


def by_core(core, mine, other, axis):
    return jnp.where(
        core == 0,
        jnp.concatenate([mine, other], axis),
        jnp.concatenate([other, mine], axis),
    )


def exchange(blocks):
    flat = blocks.reshape(blocks.shape[0] * blocks.shape[1], blocks.shape[2])
    moved = lax.all_to_all(flat, "chip", split_axis=0, concat_axis=0, tiled=True)
    return moved.reshape(blocks.shape)


def dot(a, b):
    return jnp.dot(a, b, preferred_element_type=jnp.float32)


def turn(values, cosine, sine):
    return values * cosine + pltpu.roll(values, HD // 2, 1) * sine


def project_kernel(x_ref, gain_ref, mine_ref, other_ref, pair_ref, keep_ref, give_ref):
    n_chip, rows, width = x_ref.shape
    columns = mine_ref.shape[1]
    square = jnp.zeros((rows, 1), jnp.float32)
    parts = []
    for j in range(n_chip):
        part = x_ref[j].astype(jnp.float32)
        square += jnp.sum(part * part, axis=-1, keepdims=True)
        parts.append((part * gain_ref[j : j + 1, :]).astype(jnp.bfloat16))
    scaled = jnp.concatenate(parts, axis=1)
    keep_ref[:, :columns] = dot(scaled, mine_ref[...])
    give_ref[:, :columns] = dot(scaled, other_ref[...])
    pair = dot(scaled, pair_ref[...])
    squares = jnp.broadcast_to(square, (rows, HD))
    for ref in (keep_ref, give_ref):
        ref[:, columns : columns + 2 * HD] = pair
        ref[:, columns + 2 * HD :] = squares


def attend_kernel(
    depth, where_ref, keep_ref, got_ref, cos_ref, sin_ref, held_ref, fresh_ref, attended_ref, new_ref
):
    rows, columns = attended_ref.shape
    batch, length, offset, valid = where_ref[0], where_ref[1], where_ref[2], where_ref[3]
    cached = held_ref.shape[1]
    span = fresh_ref.shape[1]
    total = keep_ref[...] + got_ref[...]
    square = total[:, columns + 2 * HD : columns + 2 * HD + 1]
    scale = lax.rsqrt(square / depth + EPS)
    cosine = cos_ref[...] * scale
    sine = sin_ref[...] * scale
    pair = total[:, columns : columns + 2 * HD]
    low = HD // 2
    keys = jnp.concatenate([pair[:, :low], pair[:, HD : HD + low]], axis=1)
    values = jnp.concatenate([pair[:, low:HD], pair[:, HD + low :]], axis=1) * scale
    new_ref[...] = fresh_ref[...]

    @pl.when(valid == 1)
    def _():
        place = pl.ds(pl.multiple_of(offset, rows), rows)
        new_ref[batch, place, :HD] = turn(keys, cosine, sine).astype(jnp.bfloat16)
        new_ref[batch, place, HD:] = values.astype(jnp.bfloat16)

    live = lax.broadcasted_iota(jnp.int32, (1, cached), 1) < length
    row = lax.broadcasted_iota(jnp.int32, (rows, span), 0) + offset
    causal = lax.broadcasted_iota(jnp.int32, (rows, span), 1) <= row
    heads = columns // HD
    group = max(1, min(heads, 128 // rows))
    causal = jnp.concatenate([causal] * group, axis=0)
    root = 1.0 / math.sqrt(HD)
    contract = (((1,), (1,)), ((), ()))
    for base in range(0, heads, group):
        queries = jnp.concatenate(
            [
                turn(total[:, h * HD : (h + 1) * HD], cosine, sine).astype(jnp.bfloat16)
                for h in range(base, base + group)
            ],
            axis=0,
        )
        scores = lax.dot_general(
            queries, held_ref[batch, :, :HD], contract, preferred_element_type=jnp.float32
        )
        scores = jnp.where(live, scores, -1e30)
        recent = lax.dot_general(
            queries, new_ref[batch, :, :HD], contract, preferred_element_type=jnp.float32
        )
        recent = jnp.where(causal, recent, -1e30)
        top = jnp.maximum(
            jnp.max(scores, axis=-1, keepdims=True), jnp.max(recent, axis=-1, keepdims=True)
        )
        scores = jnp.exp((scores - top) * root)
        recent = jnp.exp((recent - top) * root)
        weight = jnp.sum(scores, axis=-1, keepdims=True) + jnp.sum(recent, axis=-1, keepdims=True)
        mixed = dot(scores.astype(jnp.bfloat16), held_ref[batch, :, HD:]) + dot(
            recent.astype(jnp.bfloat16), new_ref[batch, :, HD:]
        )
        mixed = (mixed / weight).astype(jnp.bfloat16)
        for h in range(group):
            attended_ref[:, (base + h) * HD : (base + h + 1) * HD] = mixed[
                h * rows : (h + 1) * rows
            ]


def out_kernel(mine_ref, got_ref, own_ref, other_ref, partial_ref):
    n_chip, _, width = partial_ref.shape
    for j in range(n_chip):
        columns = slice(j * width, (j + 1) * width)
        partial = dot(mine_ref[...], own_ref[:, columns]) + dot(got_ref[...], other_ref[:, columns])
        partial_ref[j] = partial.astype(jnp.bfloat16)


def fast(x):
    return pltpu.with_memory_space_constraint(x, pltpu.VMEM)


def call(kernel, out, flops, scalars, arrays):
    return pl.pallas_call(
        kernel,
        out_shape=out,
        in_specs=[pl.BlockSpec(memory_space=pltpu.SMEM)] * scalars
        + [pl.BlockSpec(memory_space=pltpu.VMEM)] * arrays,
        out_specs=jax.tree.map(lambda _: pl.BlockSpec(memory_space=pltpu.VMEM), out),
        compiler_params=pltpu.CompilerParams(vmem_limit_bytes=LIMIT),
        cost_estimate=pl.CostEstimate(flops=flops, bytes_accessed=2**20, transcendentals=0),
    )


def shards(hidden_in, norm_gain, w_query, w_key_value, w_out, cache, ctx_len, placement):
    n_section = lax.axis_size("section")
    n_chip = lax.axis_size("chip")
    section = lax.axis_index("section")
    chip = lax.axis_index("chip")
    core = lax.axis_index("core")
    micro, span, width = hidden_in.shape
    rows = min(ROWS, span)
    parts = span // rows
    chunks = micro * parts
    steps = n_section + chunks - 1
    depth = n_chip * 2 * width
    columns = w_query.shape[2]
    bf16 = jnp.bfloat16
    inputs = hidden_in.reshape(chunks, rows, width)

    def halves(x, axis):
        keep = lax.dynamic_index_in_dim(x, core, axis, keepdims=False)
        give = lax.dynamic_index_in_dim(x, 1 - core, axis, keepdims=False)
        return keep, swap(give)

    wq_own, wq_other = halves(w_query[0].reshape(n_chip, 2, width, columns), 1)
    pair_own, pair_other = halves(w_key_value[0].reshape(n_chip, 2, width, HD), 1)
    wq_own = wq_own.reshape(depth // 2, columns)
    wq_other = wq_other.reshape(depth // 2, columns)
    w_pair = by_core(core, pair_own, pair_other, 2).reshape(depth // 2, 2 * HD)
    gain = lax.dynamic_index_in_dim(norm_gain[0].reshape(n_chip, 2, width), core, 1, keepdims=False)
    context = by_core(core, cache[0], swap(cache[0]), 1)
    wo_own, wo_other = halves(w_out[0].reshape(columns, n_chip, 2, width), 2)
    wo_own = wo_own.reshape(columns, depth // 2)
    wo_other = wo_other.reshape(columns, depth // 2)

    freqs = jnp.exp(jnp.arange(HD // 2, dtype=jnp.float32) * (-2.0 * math.log(500000.0) / HD))
    order = jnp.clip(jnp.arange(steps) - section, 0, chunks - 1)
    batches = order // parts
    offsets = (order % parts) * rows
    valids = (jnp.arange(steps) >= section) & (jnp.arange(steps) < section + chunks)
    wheres = jnp.stack(
        [batches, ctx_len[batches], offsets, valids.astype(jnp.int32)], axis=1
    ).astype(jnp.int32)
    chunk = jnp.arange(chunks)
    positions = (ctx_len[chunk // parts] + (chunk % parts) * rows)[:, None] + jnp.arange(
        rows, dtype=jnp.int32
    )
    angles = positions.astype(jnp.float32)[:, :, None] * freqs
    cosines = jnp.concatenate([jnp.cos(angles), jnp.cos(angles)], axis=-1)
    sines = jnp.concatenate([-jnp.sin(angles), jnp.sin(angles)], axis=-1)
    wq_own, wq_other, wo_own, wo_other, w_pair, context = (
        fast(v) for v in (wq_own, wq_other, wo_own, wo_other, w_pair, context)
    )
    packed = jax.ShapeDtypeStruct((rows, columns + 3 * HD), jnp.float32)
    project = call(
        project_kernel, (packed, packed), rows * depth * 2 * (columns + HD), 0, 5
    )
    attend = call(
        functools.partial(attend_kernel, depth),
        (
            jax.ShapeDtypeStruct((rows, columns), bf16),
            jax.ShapeDtypeStruct((micro, span, 2 * HD), bf16),
        ),
        4 * rows * columns * (context.shape[1] + span),
        1,
        6,
    )
    finish = call(
        out_kernel,
        jax.ShapeDtypeStruct((n_chip, rows, width), bf16),
        2 * rows * columns * depth,
        0,
        4,
    )

    incoming = None
    fresh = jnp.zeros((micro, span, 2 * HD), bf16)
    updates = []
    for step in range(steps):
        if step < chunks:
            layer_in = inputs[step]
            if step > 0:
                layer_in = jnp.where(section == 0, layer_in, incoming)
        else:
            layer_in = incoming
        features = exchange(jnp.broadcast_to(layer_in[None], (n_chip, rows, width)))
        keep, give = project(features, gain, wq_own, wq_other, w_pair)
        cosine = lax.dynamic_index_in_dim(cosines, order[step], 0, keepdims=False)
        sine = lax.dynamic_index_in_dim(sines, order[step], 0, keepdims=False)
        attended, fresh = attend(
            wheres[step], keep, swap(give), cosine, sine, context, fresh
        )
        partial = finish(attended, swap(attended), wo_own, wo_other)
        pieces = exchange(partial).astype(jnp.float32)
        updated = (layer_in.astype(jnp.float32) + jnp.sum(pieces, axis=0)).astype(bf16)
        updates.append(updated)
        if step + 1 < steps:
            incoming = lax.ppermute(
                updated, "section", [(i, i + 1) for i in range(n_section - 1)]
            )
    outputs = lax.dynamic_slice_in_dim(jnp.stack(updates), section, chunks, 0)
    outputs = outputs.reshape(micro, span, width)

    half = span // 2
    here = lax.dynamic_slice_in_dim(fresh, core * half, half, 1).reshape(1, micro * half, 2 * HD)
    blocks = exchange(jnp.broadcast_to(here, (n_chip, micro * half, 2 * HD)))
    blocks = blocks.reshape(n_chip * micro, half, 2 * HD)
    holders = placement[0].reshape(-1)
    count = holders.shape[0]
    earlier = (holders[None, :] == holders[:, None]) & (
        jnp.arange(count)[None, :] < jnp.arange(count)[:, None]
    )
    ranks = jnp.sum(earlier.astype(jnp.int32), axis=-1)

    def pick(member):
        chosen = (holders[None, :] == member) & (ranks[None, :] == jnp.arange(SLOTS)[:, None])
        found = jnp.any(chosen, axis=1)
        which = jnp.sum(chosen.astype(jnp.int32) * jnp.arange(count)[None, :], axis=1)
        return jnp.stack(
            [
                jnp.where(
                    found[s], lax.dynamic_index_in_dim(blocks, which[s], 0, keepdims=False), 0
                )
                for s in range(SLOTS)
            ]
        )

    store = by_core(core, pick(2 * chip + core), swap(pick(2 * chip + 1 - core)), 1)
    return (outputs[None], store[None])


def solution(mesh):
    n_section, n_tp = mesh.devices.shape
    fine = Mesh(mesh.devices.reshape(n_section, n_tp // 2, 2), ("section", "chip", "core"))
    tp = ("chip", "core")
    in_specs = (
        P(None, None, tp),
        P("section", None),
        P("section", None, tp),
        P("section", None, tp),
        P("section", tp, None),
        P("section", None, tp, None),
        P(),
        P("section", None, None),
    )
    out_specs = (P("section", None, None, tp), P("section", tp, None, None))
    return jax.shard_map(shards, mesh=fine, in_specs=in_specs, out_specs=out_specs, check_vma=False)
```

```python
import functools
import math

import jax
import jax.numpy as jnp
from jax import lax
from jax.experimental import pallas as pl
from jax.experimental.pallas import tpu as pltpu
from jax.sharding import Mesh
from jax.sharding import PartitionSpec as P

HD = 128
SLOTS = 2
EPS = 1e-05
ROWS = 64


def swap(x):
    return lax.ppermute(x, "core", [(0, 1), (1, 0)])


def exchange(blocks):
    flat = blocks.reshape(blocks.shape[0] * blocks.shape[1], blocks.shape[2])
    moved = lax.all_to_all(flat, "chip", split_axis=0, concat_axis=0, tiled=True)
    return moved.reshape(blocks.shape)


def dot(a, b):
    return jnp.dot(a, b, preferred_element_type=jnp.float32)


def turn(values, cosine, sine):
    return values * cosine + pltpu.roll(values, HD // 2, 1) * sine


def table_kernel(parts, ctx_ref, cos_ref, sin_ref, fresh_ref, done_ref):
    chunks, rows, _ = cos_ref.shape
    lane = lax.broadcasted_iota(jnp.int32, (1, HD), 1)
    upper = lane >= HD // 2
    index = jnp.where(upper, lane - HD // 2, lane).astype(jnp.float32)
    freqs = jnp.exp(index * (-2.0 * math.log(500000.0) / HD))
    row = lax.broadcasted_iota(jnp.int32, (rows, HD), 0)
    for c in range(chunks):
        positions = ctx_ref[c // parts] + (c % parts) * rows + row
        angles = positions.astype(jnp.float32) * freqs
        cos_ref[c] = jnp.cos(angles)
        sine = jnp.sin(angles)
        sin_ref[c] = jnp.where(upper, sine, -sine)
    fresh_ref[...] = jnp.zeros_like(fresh_ref)
    done_ref[...] = jnp.zeros_like(done_ref)


def project_kernel(x_ref, gain_ref, mine_ref, other_ref, pair_ref, keep_ref, give_ref):
    n_chip, rows, width = x_ref.shape
    columns = mine_ref.shape[1]
    square = jnp.zeros((rows, 1), jnp.float32)
    parts = []
    core = lax.axis_index("core")
    for j in range(n_chip):
        part = x_ref[j].astype(jnp.float32)
        square += jnp.sum(part * part, axis=-1, keepdims=True)
        parts.append((part * gain_ref[:, strip(j, core, width)]).astype(jnp.bfloat16))
    scaled = jnp.concatenate(parts, axis=1)
    keep_ref[:, :columns] = dot(scaled, mine_ref[...])
    give_ref[:, :columns] = dot(scaled, other_ref[...])
    pair = dot(scaled, pair_ref[...])
    squares = jnp.broadcast_to(square, (rows, HD))
    for ref in (keep_ref, give_ref):
        ref[:, columns : columns + 2 * HD] = pair
        ref[:, columns + 2 * HD :] = squares


def attend_kernel(
    depth, step, ctx_ref, keep_ref, got_ref, cos_ref, sin_ref, held_ref, fresh_ref, attended_ref,
    new_ref,
):
    rows, columns = attended_ref.shape
    chunks, parts = cos_ref.shape[0], new_ref.shape[1] // rows
    index = step - lax.axis_index("section")
    valid = jnp.logical_and(index >= 0, index < chunks)
    index = jnp.clip(index, 0, chunks - 1)
    batch, offset = index // parts, (index % parts) * rows
    length = ctx_ref[batch]
    cached = held_ref.shape[1]
    span = fresh_ref.shape[1]
    total = keep_ref[...] + got_ref[...]
    square = total[:, columns + 2 * HD : columns + 2 * HD + 1]
    scale = lax.rsqrt(square / depth + EPS)
    cosine = cos_ref[index] * scale
    sine = sin_ref[index] * scale
    pair = total[:, columns : columns + 2 * HD]
    low = HD // 2
    keys = jnp.concatenate([pair[:, :low], pair[:, HD : HD + low]], axis=1)
    values = jnp.concatenate([pair[:, low:HD], pair[:, HD + low :]], axis=1) * scale
    new_ref[...] = fresh_ref[...]

    @pl.when(valid)
    def _():
        place = pl.ds(pl.multiple_of(offset, rows), rows)
        new_ref[batch, place, :HD] = turn(keys, cosine, sine).astype(jnp.bfloat16)
        new_ref[batch, place, HD:] = values.astype(jnp.bfloat16)

    live = lax.broadcasted_iota(jnp.int32, (1, cached), 1) < length
    row = lax.broadcasted_iota(jnp.int32, (rows, span), 0) + offset
    causal = lax.broadcasted_iota(jnp.int32, (rows, span), 1) <= row
    heads = columns // HD
    group = max(1, min(heads, 128 // rows))
    causal = jnp.concatenate([causal] * group, axis=0)
    root = 1.0 / math.sqrt(HD)
    contract = (((1,), (1,)), ((), ()))
    for base in range(0, heads, group):
        queries = jnp.concatenate(
            [
                turn(total[:, h * HD : (h + 1) * HD], cosine, sine).astype(jnp.bfloat16)
                for h in range(base, base + group)
            ],
            axis=0,
        )
        scores = lax.dot_general(
            queries, held_ref[batch, :, :HD], contract, preferred_element_type=jnp.float32
        )
        scores = jnp.where(live, scores, -1e30)
        recent = lax.dot_general(
            queries, new_ref[batch, :, :HD], contract, preferred_element_type=jnp.float32
        )
        recent = jnp.where(causal, recent, -1e30)
        top = jnp.maximum(
            jnp.max(scores, axis=-1, keepdims=True), jnp.max(recent, axis=-1, keepdims=True)
        )
        scores = jnp.exp((scores - top) * root)
        recent = jnp.exp((recent - top) * root)
        weight = jnp.sum(scores, axis=-1, keepdims=True) + jnp.sum(recent, axis=-1, keepdims=True)
        mixed = dot(scores.astype(jnp.bfloat16), held_ref[batch, :, HD:]) + dot(
            recent.astype(jnp.bfloat16), new_ref[batch, :, HD:]
        )
        mixed = (mixed / weight).astype(jnp.bfloat16)
        for h in range(group):
            attended_ref[:, (base + h) * HD : (base + h + 1) * HD] = mixed[
                h * rows : (h + 1) * rows
            ]


def out_kernel(mine_ref, got_ref, own_ref, other_ref, partial_ref):
    n_chip, _, width = partial_ref.shape
    for j in range(n_chip):
        columns = slice(j * width, (j + 1) * width)
        partial = dot(mine_ref[...], own_ref[:, columns]) + dot(got_ref[...], other_ref[:, columns])
        partial_ref[j] = partial.astype(jnp.bfloat16)


def enter_kernel(step, incoming_ref, inputs_ref, layer_ref, copies_ref):
    layer_ref[...] = incoming_ref[...]

    @pl.when(lax.axis_index("section") == 0)
    def _():
        layer_ref[...] = inputs_ref[step]

    for j in range(copies_ref.shape[0]):
        copies_ref[j] = layer_ref[...]


def settle_kernel(step, pieces_ref, layer_ref, done_ref, send_ref, new_ref):
    chunks = done_ref.shape[0]
    section = lax.axis_index("section")
    index = step - section
    total = layer_ref[...].astype(jnp.float32)
    summed = pieces_ref[0].astype(jnp.float32)
    for j in range(1, pieces_ref.shape[0]):
        summed += pieces_ref[j].astype(jnp.float32)
    updated = (total + summed).astype(jnp.bfloat16)
    send_ref[...] = updated
    new_ref[...] = done_ref[...]

    @pl.when(jnp.logical_and(index >= 0, index < chunks))
    def _():
        new_ref[jnp.clip(index, 0, chunks - 1)] = updated


def share_kernel(fresh_ref, copies_ref):
    micro, span, _ = fresh_ref.shape
    half = span // 2
    rows = pl.ds(pl.multiple_of(lax.axis_index("core") * half, half), half)
    for m in range(micro):
        block = fresh_ref[m, rows, :]
        for j in range(copies_ref.shape[0]):
            copies_ref[j, m * half : (m + 1) * half, :] = block


def pick_kernel(holders_ref, blocks_ref, mine_ref, other_ref):
    heads, micro = holders_ref.shape
    count = heads * micro
    half = mine_ref.shape[1]
    holders = [holders_ref[e // micro, e % micro] for e in range(count)]
    core = lax.axis_index("core")
    first = 2 * lax.axis_index("chip")
    for ref, member in ((mine_ref, first + core), (other_ref, first + 1 - core)):
        ref[...] = jnp.zeros_like(ref)
        slot = jnp.int32(0)
        for e in range(count):
            here = holders[e] == member

            @pl.when(here)
            def _(slot=slot, e=e, ref=ref):
                ref[slot] = blocks_ref[e // micro, (e % micro) * half : (e % micro + 1) * half, :]

            slot = jnp.minimum(slot + here.astype(jnp.int32), SLOTS - 1)


def move(copies, sems):
    started = [
        pltpu.make_async_copy(source, target, sems.at[i])
        for i, (source, target) in enumerate(copies)
    ]
    for copy in started:
        copy.start()
    for copy in started:
        copy.wait()


def strip(chip, core, width):
    return pl.ds(pl.multiple_of((2 * chip + core) * width, width), width)


def give_kernel(width, query_ref, pair_ref, give_query_ref, give_pair_ref, sems):
    other = 1 - lax.axis_index("core")
    copies = []
    for j in range(query_ref.shape[0] // (2 * width)):
        rows, here = strip(j, other, width), pl.ds(j * width, width)
        copies.append((query_ref.at[rows], give_query_ref.at[here]))
        copies.append((pair_ref.at[rows], give_pair_ref.at[here]))
    move(copies, sems)


def keep_kernel(width, query_ref, out_ref, own_query_ref, own_out_ref, give_out_ref, sems):
    core = lax.axis_index("core")
    copies = []
    for j in range(query_ref.shape[0] // (2 * width)):
        mine, here = strip(j, core, width), pl.ds(j * width, width)
        copies.append((query_ref.at[mine], own_query_ref.at[here]))
        copies.append((out_ref.at[:, mine], own_out_ref.at[:, here]))
        copies.append((out_ref.at[:, strip(j, 1 - core, width)], give_out_ref.at[:, here]))
    move(copies, sems)


def join_kernel(
    n_chip, pair_ref, got_pair_ref, cache_ref, got_cache_ref, got_query_ref,
    both_ref, context_ref, other_query_ref, sems,
):
    width = pair_ref.shape[0] // (2 * n_chip)
    core = lax.axis_index("core")
    length = cache_ref.shape[1]
    mine, theirs = pl.ds(pl.multiple_of(core * HD, HD), HD), pl.ds(pl.multiple_of((1 - core) * HD, HD), HD)
    early = pl.ds(pl.multiple_of(core * length, length), length)
    late = pl.ds(pl.multiple_of((1 - core) * length, length), length)
    copies = [
        (got_pair_ref, both_ref.at[:, theirs]),
        (cache_ref, context_ref.at[:, early]),
        (got_cache_ref, context_ref.at[:, late]),
        (got_query_ref, other_query_ref),
    ]
    for j in range(n_chip):
        copies.append(
            (pair_ref.at[strip(j, core, width)], both_ref.at[pl.ds(j * width, width), mine])
        )
    move(copies, sems)


def load_kernel(source_ref, target_ref, sems):
    move([(source_ref, target_ref)], sems)


def shuffle(kernel, out, inputs, copies):
    return pl.pallas_call(
        kernel,
        out_shape=out,
        in_specs=[pl.BlockSpec(memory_space=pl.ANY)] * inputs,
        out_specs=jax.tree.map(lambda _: pl.BlockSpec(memory_space=pl.ANY), out),
        scratch_shapes=[pltpu.SemaphoreType.DMA((copies,))],
        compiler_params=pltpu.CompilerParams(vmem_limit_bytes=2**20),
    )


def fast(x):
    return pltpu.with_memory_space_constraint(x, pltpu.VMEM)


def slow(x):
    return pltpu.with_memory_space_constraint(x, pltpu.HBM)


def call(kernel, out, flops, scalars, arrays, limit):
    return pl.pallas_call(
        kernel,
        out_shape=out,
        in_specs=[pl.BlockSpec(memory_space=pltpu.SMEM)] * scalars
        + [pl.BlockSpec(memory_space=pltpu.VMEM)] * arrays,
        out_specs=jax.tree.map(lambda _: pl.BlockSpec(memory_space=pltpu.VMEM), out),
        compiler_params=pltpu.CompilerParams(vmem_limit_bytes=limit * 2**20),
        cost_estimate=pl.CostEstimate(flops=flops, bytes_accessed=2**20, transcendentals=0),
    )


def shards(hidden_in, norm_gain, w_query, w_key_value, w_out, cache, ctx_len, placement):
    n_section = lax.axis_size("section")
    n_chip = lax.axis_size("chip")
    micro, span, width = hidden_in.shape
    rows = min(ROWS, span)
    parts = span // rows
    chunks = micro * parts
    steps = n_section + chunks - 1
    depth = n_chip * 2 * width
    side = depth // 2
    columns = w_query.shape[2]
    bf16, f32 = jnp.bfloat16, jnp.float32
    shape = jax.ShapeDtypeStruct

    def vmem(*dims):
        return pltpu.VMEM(dims, bf16)

    wq, wkv, wo, held = (slow(x[0]) for x in (w_query, w_key_value, w_out, cache))
    inputs = fast(hidden_in.reshape(chunks, rows, width))
    gain = fast(norm_gain)
    angle = shape((chunks, rows, HD), f32)
    state = shape((micro, span, 2 * HD), bf16)
    done_shape = shape((chunks, rows, width), bf16)
    cosines, sines, fresh, done = call(
        functools.partial(table_kernel, parts), (angle, angle, state, done_shape), 2**20, 1, 0, 4
    )(ctx_len)

    give_query, give_pair = shuffle(
        functools.partial(give_kernel, width), (vmem(side, columns), vmem(side, HD)), 2, 2 * n_chip
    )(wq, wkv)
    got_query, got_pair, got_cache = swap(give_query), swap(give_pair), swap(cache[0])
    layer_in, cosines, sines, fresh, done, _ = lax.optimization_barrier(
        (hidden_in[0, :rows], cosines, sines, fresh, done, give_query)
    )
    features = exchange(jnp.broadcast_to(layer_in[None], (n_chip, rows, width)))
    features, w_query, w_out = lax.optimization_barrier((features, w_query, w_out))
    wq, wo = slow(w_query[0]), slow(w_out[0])
    wq_own, wo_own, give_out = shuffle(
        functools.partial(keep_kernel, width),
        (vmem(side, columns), vmem(columns, side), vmem(columns, side)),
        2,
        3 * n_chip,
    )(wq, wo)
    got_out = swap(give_out)
    w_pair, context, wq_other = shuffle(
        functools.partial(join_kernel, n_chip),
        (vmem(side, 2 * HD), vmem(micro, 2 * cache.shape[2], 2 * HD), vmem(side, columns)),
        5,
        4 + n_chip,
    )(wkv, slow(got_pair), held, slow(got_cache), slow(got_query))
    wo_other = None
    wq_own, wo_own, w_pair, context, wq_other = (
        fast(v) for v in (wq_own, wo_own, w_pair, context, wq_other)
    )

    packed = shape((rows, columns + 3 * HD), f32)
    block = shape((rows, columns), bf16)
    project = call(
        project_kernel, (packed, packed), rows * depth * 2 * (columns + HD), 0, 5, 4
    )
    finish = call(
        out_kernel, shape((n_chip, rows, width), bf16), 2 * rows * columns * depth, 0, 4, 4
    )
    for step in range(steps):
        if step > 0:
            if step < chunks:
                layer_in, copies = call(
                    functools.partial(enter_kernel, step),
                    (block, shape((n_chip, rows, width), bf16)),
                    2**20,
                    0,
                    2,
                    4,
                )(layer_in, inputs)
            else:
                copies = jnp.broadcast_to(layer_in[None], (n_chip, rows, width))
            features = exchange(copies)
        keep, give = project(features, gain, wq_own, wq_other, w_pair)
        attend = call(
            functools.partial(attend_kernel, depth, step),
            (block, state),
            4 * rows * columns * (context.shape[1] + span),
            1,
            6,
            12,
        )
        attended, fresh = attend(ctx_len, keep, swap(give), cosines, sines, context, fresh)
        if step == 0:
            wo_other = fast(shuffle(load_kernel, vmem(columns, side), 1, 1)(slow(got_out)))
        partial = finish(attended, swap(attended), wo_own, wo_other)
        if step + 1 == steps:
            partial, fresh = lax.optimization_barrier((partial, fresh))
            copies = call(
                share_kernel, shape((n_chip, micro * span // 2, 2 * HD), bf16), 2**20, 0, 1, 4
            )(fresh)
            blocks = exchange(copies)
        pieces = exchange(partial)
        settle = call(
            functools.partial(settle_kernel, step), (block, done_shape), 2**20, 0, 3, 4
        )
        send, done = settle(pieces, layer_in, done)
        if step + 1 < steps:
            route = [
                (i, i + 1)
                for i in range(max(0, step - chunks + 1), min(step, n_section - 2) + 1)
            ]
            layer_in = lax.ppermute(send, "section", route)
    outputs = done.reshape(micro, span, width)

    slots = shape((SLOTS, span // 2, 2 * HD), bf16)
    mine, other = call(pick_kernel, (slots, slots), 2**20, 1, 1, 4)(placement[0], blocks)
    other = swap(other)
    store = jnp.where(
        lax.axis_index("core") == 0,
        jnp.concatenate([mine, other], axis=1),
        jnp.concatenate([other, mine], axis=1),
    )
    return (outputs[None], store[None])


def solution(mesh):
    n_section, n_tp = mesh.devices.shape
    fine = Mesh(mesh.devices.reshape(n_section, n_tp // 2, 2), ("section", "chip", "core"))
    tp = ("chip", "core")
    in_specs = (
        P(None, None, tp),
        P("section", None),
        P("section", None, tp),
        P("section", None, tp),
        P("section", tp, None),
        P("section", None, tp, None),
        P(),
        P("section", None, None),
    )
    out_specs = (P("section", None, None, tp), P("section", tp, None, None))
    return jax.shard_map(shards, mesh=fine, in_specs=in_specs, out_specs=out_specs, check_vma=False)
```

```python
import functools
import math

import jax
import jax.numpy as jnp
from jax import lax
from jax.experimental import pallas as pl
from jax.experimental.pallas import tpu as pltpu
from jax.sharding import Mesh
from jax.sharding import PartitionSpec as P

HD = 128
SLOTS = 2
EPS = 1e-05
ROWS = 64


def swap(x):
    return lax.ppermute(x, "core", [(0, 1), (1, 0)])


def exchange(blocks):
    flat = blocks.reshape(blocks.shape[0] * blocks.shape[1], blocks.shape[2])
    moved = lax.all_to_all(flat, "chip", split_axis=0, concat_axis=0, tiled=True)
    return moved.reshape(blocks.shape)


def dot(a, b):
    return jnp.dot(a, b, preferred_element_type=jnp.float32)


def turn(values, cosine, sine):
    return values * cosine + pltpu.roll(values, HD // 2, 1) * sine


def table_kernel(
    parts, ctx_ref, inputs_ref, cos_ref, sin_ref, fresh_ref, done_ref, layer_ref, copies_ref
):
    chunks, rows, _ = cos_ref.shape
    lane = lax.broadcasted_iota(jnp.int32, (1, HD), 1)
    upper = lane >= HD // 2
    index = jnp.where(upper, lane - HD // 2, lane).astype(jnp.float32)
    freqs = jnp.exp(index * (-2.0 * math.log(500000.0) / HD))
    row = lax.broadcasted_iota(jnp.int32, (rows, HD), 0)
    for c in range(chunks):
        positions = ctx_ref[c // parts] + (c % parts) * rows + row
        angles = positions.astype(jnp.float32) * freqs
        cos_ref[c] = jnp.cos(angles)
        sine = jnp.sin(angles)
        sin_ref[c] = jnp.where(upper, sine, -sine)
    fresh_ref[...] = jnp.zeros_like(fresh_ref)
    done_ref[...] = jnp.zeros_like(done_ref)
    layer_ref[...] = inputs_ref[0]
    for j in range(copies_ref.shape[0]):
        copies_ref[j] = inputs_ref[0]


def project_kernel(x_ref, gain_ref, other_ref, pair_ref, scaled_ref, give_ref):
    n_chip, rows, width = x_ref.shape
    columns = other_ref.shape[1]
    core = lax.axis_index("core")
    square = jnp.zeros((rows, 1), jnp.float32)
    for j in range(n_chip):
        part = x_ref[j].astype(jnp.float32)
        square += jnp.sum(part * part, axis=-1, keepdims=True)
        scaled_ref[:, j * width : (j + 1) * width] = (
            part * gain_ref[:, strip(j, core, width)]
        ).astype(jnp.bfloat16)
    scaled = scaled_ref[...]
    give_ref[:, :columns] = dot(scaled, other_ref[...])
    give_ref[:, columns : columns + 2 * HD] = dot(scaled, pair_ref[...])
    give_ref[:, columns + 2 * HD :] = jnp.broadcast_to(square, (rows, HD))


def query_kernel(scaled_ref, own_ref, keep_ref):
    keep_ref[...] = dot(scaled_ref[...], own_ref[...])


def attend_kernel(
    depth, step, ctx_ref, keep_ref, give_ref, got_ref, cos_ref, sin_ref, held_ref, fresh_ref, attended_ref,
    new_ref,
):
    rows, columns = attended_ref.shape
    chunks, parts = cos_ref.shape[0], new_ref.shape[1] // rows
    index = step - lax.axis_index("section")
    valid = jnp.logical_and(index >= 0, index < chunks)
    index = jnp.clip(index, 0, chunks - 1)
    batch, offset = index // parts, (index % parts) * rows
    length = ctx_ref[batch]
    cached = held_ref.shape[1]
    span = fresh_ref.shape[1]
    total = keep_ref[...] + got_ref[:, :columns]
    rest = give_ref[:, columns:] + got_ref[:, columns:]
    square = rest[:, 2 * HD : 2 * HD + 1]
    scale = lax.rsqrt(square / depth + EPS)
    cosine = cos_ref[index] * scale
    sine = sin_ref[index] * scale
    pair = rest[:, : 2 * HD]
    low = HD // 2
    keys = jnp.concatenate([pair[:, :low], pair[:, HD : HD + low]], axis=1)
    values = jnp.concatenate([pair[:, low:HD], pair[:, HD + low :]], axis=1) * scale
    new_ref[...] = fresh_ref[...]

    @pl.when(valid)
    def _():
        place = pl.ds(pl.multiple_of(offset, rows), rows)
        new_ref[batch, place, :HD] = turn(keys, cosine, sine).astype(jnp.bfloat16)
        new_ref[batch, place, HD:] = values.astype(jnp.bfloat16)

    live = lax.broadcasted_iota(jnp.int32, (1, cached), 1) < length
    row = lax.broadcasted_iota(jnp.int32, (rows, span), 0) + offset
    causal = lax.broadcasted_iota(jnp.int32, (rows, span), 1) <= row
    heads = columns // HD
    group = max(1, min(heads, 128 // rows))
    causal = jnp.concatenate([causal] * group, axis=0)
    root = 1.0 / math.sqrt(HD)
    contract = (((1,), (1,)), ((), ()))
    for base in range(0, heads, group):
        queries = jnp.concatenate(
            [
                turn(total[:, h * HD : (h + 1) * HD], cosine, sine).astype(jnp.bfloat16)
                for h in range(base, base + group)
            ],
            axis=0,
        )
        scores = lax.dot_general(
            queries, held_ref[batch, :, :HD], contract, preferred_element_type=jnp.float32
        )
        scores = jnp.where(live, scores, -1e30)
        recent = lax.dot_general(
            queries, new_ref[batch, :, :HD], contract, preferred_element_type=jnp.float32
        )
        recent = jnp.where(causal, recent, -1e30)
        top = jnp.maximum(
            jnp.max(scores, axis=-1, keepdims=True), jnp.max(recent, axis=-1, keepdims=True)
        )
        scores = jnp.exp((scores - top) * root)
        recent = jnp.exp((recent - top) * root)
        weight = jnp.sum(scores, axis=-1, keepdims=True) + jnp.sum(recent, axis=-1, keepdims=True)
        mixed = dot(scores.astype(jnp.bfloat16), held_ref[batch, :, HD:]) + dot(
            recent.astype(jnp.bfloat16), new_ref[batch, :, HD:]
        )
        mixed = (mixed / weight).astype(jnp.bfloat16)
        for h in range(group):
            attended_ref[:, (base + h) * HD : (base + h + 1) * HD] = mixed[
                h * rows : (h + 1) * rows
            ]


def out_kernel(mine_ref, own_ref, part_ref):
    width = part_ref.shape[2]
    for j in range(part_ref.shape[0]):
        part_ref[j] = dot(mine_ref[...], own_ref[:, j * width : (j + 1) * width])


def finish_kernel(part_ref, got_ref, other_ref, partial_ref):
    width = part_ref.shape[2]
    for j in range(part_ref.shape[0]):
        more = dot(got_ref[...], other_ref[:, j * width : (j + 1) * width])
        partial_ref[j] = (part_ref[j] + more).astype(jnp.bfloat16)


def last_kernel(part_ref, got_ref, other_ref, fresh_ref, partial_ref):
    n_chip, rows, width = part_ref.shape
    micro, span, depth = fresh_ref.shape
    half = span // 2
    place = pl.ds(pl.multiple_of(lax.axis_index("core") * half, half), half)
    for j in range(n_chip):
        more = dot(got_ref[...], other_ref[:, j * width : (j + 1) * width])
        partial_ref[j, :rows] = (part_ref[j] + more).astype(jnp.bfloat16)
        for m in range(micro):
            partial_ref[j, rows:, m * depth : (m + 1) * depth] = fresh_ref[m, place, :]


def enter_kernel(step, incoming_ref, inputs_ref, layer_ref, copies_ref):
    layer_ref[...] = incoming_ref[...]

    @pl.when(lax.axis_index("section") == 0)
    def _():
        layer_ref[...] = inputs_ref[step]

    for j in range(copies_ref.shape[0]):
        copies_ref[j] = layer_ref[...]


def settle_kernel(step, pieces_ref, layer_ref, done_ref, send_ref, new_ref):
    chunks = done_ref.shape[0]
    section = lax.axis_index("section")
    index = step - section
    total = layer_ref[...].astype(jnp.float32)
    rows = layer_ref.shape[0]
    summed = pieces_ref[0, :rows].astype(jnp.float32)
    for j in range(1, pieces_ref.shape[0]):
        summed += pieces_ref[j, :rows].astype(jnp.float32)
    updated = (total + summed).astype(jnp.bfloat16)
    send_ref[...] = updated
    new_ref[...] = done_ref[...]

    @pl.when(jnp.logical_and(index >= 0, index < chunks))
    def _():
        new_ref[jnp.clip(index, 0, chunks - 1)] = updated


def pick_kernel(holders_ref, blocks_ref, mine_ref, other_ref):
    heads, micro = holders_ref.shape
    count = heads * micro
    _, half, depth = mine_ref.shape
    below = blocks_ref.shape[1] - half
    holders = [holders_ref[e // micro, e % micro] for e in range(count)]
    core = lax.axis_index("core")
    first = 2 * lax.axis_index("chip")
    for ref, member in ((mine_ref, first + core), (other_ref, first + 1 - core)):
        ref[...] = jnp.zeros_like(ref)
        slot = jnp.int32(0)
        for e in range(count):
            here = holders[e] == member

            @pl.when(here)
            def _(slot=slot, e=e, ref=ref):
                ref[slot] = blocks_ref[
                    e // micro, below:, (e % micro) * depth : (e % micro + 1) * depth
                ]

            slot = jnp.minimum(slot + here.astype(jnp.int32), SLOTS - 1)


def move(copies, sems):
    started = [
        pltpu.make_async_copy(source, target, sems.at[i])
        for i, (source, target) in enumerate(copies)
    ]
    for copy in started:
        copy.start()
    for copy in started:
        copy.wait()


def strip(chip, core, width):
    return pl.ds(pl.multiple_of((2 * chip + core) * width, width), width)


def give_kernel(width, query_ref, pair_ref, cache_ref, out_ref, first_ref, second_ref, sems):
    other = 1 - lax.axis_index("core")
    columns = query_ref.shape[1]
    micro, length, depth = cache_ref.shape
    n_chip = query_ref.shape[0] // (2 * width)
    copies = []
    for j in range(n_chip):
        theirs, here = strip(j, other, width), pl.ds(j * width, width)
        copies.append((query_ref.at[theirs], first_ref.at[here, pl.ds(0, columns)]))
        copies.append((pair_ref.at[theirs], first_ref.at[here, pl.ds(columns, HD)]))
        copies.append((out_ref.at[:, theirs], second_ref.at[:, here]))
    for m in range(micro):
        place = first_ref.at[pl.ds(n_chip * width, length), pl.ds(m * depth, depth)]
        copies.append((cache_ref.at[m], place))
    move(copies, sems)


def keep_kernel(
    width, query_ref, pair_ref, cache_ref, out_ref, got_ref,
    own_query_ref, other_query_ref, both_ref, context_ref, own_out_ref, sems,
):
    core = lax.axis_index("core")
    columns = query_ref.shape[1]
    micro, length, depth = cache_ref.shape
    n_chip = query_ref.shape[0] // (2 * width)
    side = pl.ds(0, n_chip * width)
    own = pl.ds(pl.multiple_of(core * HD, HD), HD)
    other = pl.ds(pl.multiple_of((1 - core) * HD, HD), HD)
    early = pl.ds(pl.multiple_of(core * length, length), length)
    late = pl.ds(pl.multiple_of((1 - core) * length, length), length)
    copies = [
        (got_ref.at[side, pl.ds(0, columns)], other_query_ref),
        (got_ref.at[side, pl.ds(columns, HD)], both_ref.at[:, other]),
    ]
    for m in range(micro):
        got = got_ref.at[pl.ds(n_chip * width, length), pl.ds(m * depth, depth)]
        copies.append((got, context_ref.at[m, late]))
        copies.append((cache_ref.at[m], context_ref.at[m, early]))
    for j in range(n_chip):
        mine, here = strip(j, core, width), pl.ds(j * width, width)
        copies.append((query_ref.at[mine], own_query_ref.at[here]))
        copies.append((pair_ref.at[mine], both_ref.at[here, own]))
        copies.append((out_ref.at[:, mine], own_out_ref.at[:, here]))
    move(copies, sems)


def load_kernel(source_ref, target_ref, sems):
    move([(source_ref, target_ref)], sems)


def shuffle(kernel, out, inputs, copies):
    return pl.pallas_call(
        kernel,
        out_shape=out,
        in_specs=[pl.BlockSpec(memory_space=pl.ANY)] * inputs,
        out_specs=jax.tree.map(lambda _: pl.BlockSpec(memory_space=pl.ANY), out),
        scratch_shapes=[pltpu.SemaphoreType.DMA((copies,))],
        compiler_params=pltpu.CompilerParams(vmem_limit_bytes=2**20),
    )


def fast(x):
    return pltpu.with_memory_space_constraint(x, pltpu.VMEM)


def slow(x):
    return pltpu.with_memory_space_constraint(x, pltpu.HBM)


def call(kernel, out, flops, scalars, arrays, limit):
    return pl.pallas_call(
        kernel,
        out_shape=out,
        in_specs=[pl.BlockSpec(memory_space=pltpu.SMEM)] * scalars
        + [pl.BlockSpec(memory_space=pltpu.VMEM)] * arrays,
        out_specs=jax.tree.map(lambda _: pl.BlockSpec(memory_space=pltpu.VMEM), out),
        compiler_params=pltpu.CompilerParams(vmem_limit_bytes=limit * 2**20),
        cost_estimate=pl.CostEstimate(flops=flops, bytes_accessed=2**20, transcendentals=0),
    )


def shards(hidden_in, norm_gain, w_query, w_key_value, w_out, cache, ctx_len, placement):
    n_section = lax.axis_size("section")
    n_chip = lax.axis_size("chip")
    micro, span, width = hidden_in.shape
    rows = min(ROWS, span)
    parts = span // rows
    chunks = micro * parts
    steps = n_section + chunks - 1
    depth = n_chip * 2 * width
    side = depth // 2
    columns = w_query.shape[2]
    bf16, f32 = jnp.bfloat16, jnp.float32
    shape = jax.ShapeDtypeStruct

    def vmem(*dims):
        return pltpu.VMEM(dims, bf16)

    wq, wkv, wo, held = (slow(x[0]) for x in (w_query, w_key_value, w_out, cache))
    inputs = fast(hidden_in.reshape(chunks, rows, width))
    gain = fast(norm_gain)
    angle = shape((chunks, rows, HD), f32)
    state = shape((micro, span, 2 * HD), bf16)
    done_shape = shape((chunks, rows, width), bf16)
    packed = shape((rows, columns + 3 * HD), f32)
    block = shape((rows, columns), bf16)
    spread = shape((n_chip, rows, width), bf16)
    cosines, sines, fresh, done, layer_in, copies = call(
        functools.partial(table_kernel, parts),
        (angle, angle, state, done_shape, block, spread),
        2**20,
        1,
        1,
        4,
    )(ctx_len, inputs)

    first, second = shuffle(
        functools.partial(give_kernel, width),
        (vmem(side + cache.shape[2], columns + HD), vmem(columns, side)),
        4,
        3 * n_chip + micro,
    )(wq, wkv, held, wo)
    first, second, copies = lax.optimization_barrier((first, second, copies))
    got_first, got_second = swap(first), swap(second)
    features = exchange(copies)
    features, w_query, w_key_value, w_out, cache = lax.optimization_barrier(
        (features, w_query, w_key_value, w_out, cache)
    )
    wq, wkv, wo, held = (slow(x[0]) for x in (w_query, w_key_value, w_out, cache))
    wq_own, wq_other, w_pair, context, wo_own = shuffle(
        functools.partial(keep_kernel, width),
        (
            vmem(side, columns),
            vmem(side, columns),
            vmem(side, 2 * HD),
            vmem(micro, 2 * cache.shape[2], 2 * HD),
            vmem(columns, side),
        ),
        5,
        3 * n_chip + 2 + 2 * micro,
    )(wq, wkv, held, wo, got_first)
    wo_other = None
    wq_own, wo_own, w_pair, context, wq_other = (
        fast(v) for v in (wq_own, wo_own, w_pair, context, wq_other)
    )

    query_flops = rows * depth * columns
    project = call(
        project_kernel,
        (shape((rows, side), bf16), packed),
        query_flops + rows * depth * 2 * HD,
        0,
        4,
        4,
    )
    query = call(query_kernel, shape((rows, columns), f32), query_flops, 0, 2, 4)
    out = call(out_kernel, shape((n_chip, rows, width), f32), query_flops, 0, 2, 4)
    finish = call(finish_kernel, spread, query_flops, 0, 3, 4)
    last = call(
        last_kernel, shape((n_chip, rows + span // 2, width), bf16), query_flops, 0, 4, 4
    )
    for step in range(steps):
        if step > 0:
            if step < chunks:
                layer_in, copies = call(
                    functools.partial(enter_kernel, step),
                    (block, spread),
                    2**20,
                    0,
                    2,
                    4,
                )(layer_in, inputs)
            else:
                copies = jnp.broadcast_to(layer_in[None], (n_chip, rows, width))
            features = exchange(copies)
        scaled, give = project(features, gain, wq_other, w_pair)
        got = swap(give)
        keep = query(scaled, wq_own)
        attend = call(
            functools.partial(attend_kernel, depth, step),
            (block, state),
            4 * rows * columns * (context.shape[1] + span),
            1,
            7,
            12,
        )
        attended, fresh = attend(ctx_len, keep, give, got, cosines, sines, context, fresh)
        got = swap(attended)
        part = out(attended, wo_own)
        if step == 0:
            wo_other = fast(shuffle(load_kernel, vmem(columns, side), 1, 1)(got_second))
        if step + 1 < steps:
            pieces = exchange(finish(part, got, wo_other))
        else:
            pieces = exchange(last(part, got, wo_other, fresh))
        settle = call(
            functools.partial(settle_kernel, step), (block, done_shape), 2**20, 0, 3, 4
        )
        send, done = settle(pieces, layer_in, done)
        if step + 1 < steps:
            route = [
                (i, i + 1)
                for i in range(max(0, step - chunks + 1), min(step, n_section - 2) + 1)
            ]
            layer_in = lax.ppermute(send, "section", route)
    outputs = done.reshape(micro, span, width)

    slots = shape((SLOTS, span // 2, 2 * HD), bf16)
    mine, other = call(pick_kernel, (slots, slots), 2**20, 1, 1, 4)(placement[0], pieces)
    other = swap(other)
    store = jnp.where(
        lax.axis_index("core") == 0,
        jnp.concatenate([mine, other], axis=1),
        jnp.concatenate([other, mine], axis=1),
    )
    return (outputs[None], store[None])


def solution(mesh):
    n_section, n_tp = mesh.devices.shape
    fine = Mesh(mesh.devices.reshape(n_section, n_tp // 2, 2), ("section", "chip", "core"))
    tp = ("chip", "core")
    in_specs = (
        P(None, None, tp),
        P("section", None),
        P("section", None, tp),
        P("section", None, tp),
        P("section", tp, None),
        P("section", None, tp, None),
        P(),
        P("section", None, None),
    )
    out_specs = (P("section", None, None, tp), P("section", tp, None, None))
    return jax.shard_map(shards, mesh=fine, in_specs=in_specs, out_specs=out_specs, check_vma=False)
```

```python
import functools
import math

import jax
import jax.numpy as jnp
from jax import lax
from jax.experimental import pallas as pl
from jax.experimental.pallas import tpu as pltpu
from jax.sharding import Mesh
from jax.sharding import PartitionSpec as P

HD = 128
SLOTS = 2
EPS = 1e-05
ROWS = 64
TALL = 128


def swap(x):
    return lax.ppermute(x, "core", [(0, 1), (1, 0)])


def exchange(blocks):
    flat = blocks.reshape(blocks.shape[0] * blocks.shape[1], blocks.shape[2])
    moved = lax.all_to_all(flat, "chip", split_axis=0, concat_axis=0, tiled=True)
    return moved.reshape(blocks.shape)


def dot(a, b):
    return jnp.dot(a, b, preferred_element_type=jnp.float32)


def tall_dot(a, b):
    rows = a.shape[0]
    if rows >= TALL:
        return dot(a, b)
    return dot(jnp.concatenate([a, jnp.zeros((TALL - rows, a.shape[1]), a.dtype)], axis=0), b)[:rows]


def turn(values, cosine, sine):
    return values * cosine + pltpu.roll(values, HD // 2, 1) * sine


def table_kernel(
    parts, ctx_ref, inputs_ref, cos_ref, sin_ref, fresh_ref, done_ref, layer_ref, copies_ref
):
    chunks, rows, _ = cos_ref.shape
    lane = lax.broadcasted_iota(jnp.int32, (1, HD), 1)
    upper = lane >= HD // 2
    index = jnp.where(upper, lane - HD // 2, lane).astype(jnp.float32)
    freqs = jnp.exp(index * (-2.0 * math.log(500000.0) / HD))
    row = lax.broadcasted_iota(jnp.int32, (rows, HD), 0)
    for c in range(chunks):
        positions = ctx_ref[c // parts] + (c % parts) * rows + row
        angles = positions.astype(jnp.float32) * freqs
        cos_ref[c] = jnp.cos(angles)
        sine = jnp.sin(angles)
        sin_ref[c] = jnp.where(upper, sine, -sine)
    fresh_ref[...] = jnp.zeros_like(fresh_ref)
    done_ref[...] = jnp.zeros_like(done_ref)
    layer_ref[...] = inputs_ref[0]
    for j in range(copies_ref.shape[0]):
        copies_ref[j] = inputs_ref[0]


def project_kernel(x_ref, gain_ref, other_ref, pair_ref, scaled_ref, give_ref):
    n_chip, rows, width = x_ref.shape
    columns = other_ref.shape[1]
    core = lax.axis_index("core")
    square = jnp.zeros((rows, 1), jnp.float32)
    for j in range(n_chip):
        part = x_ref[j].astype(jnp.float32)
        square += jnp.sum(part * part, axis=-1, keepdims=True)
        scaled_ref[:, j * width : (j + 1) * width] = (
            part * gain_ref[:, strip(j, core, width)]
        ).astype(jnp.bfloat16)
    scaled = scaled_ref[...]
    give_ref[:, :columns] = tall_dot(scaled, other_ref[...])
    give_ref[:, columns : columns + 2 * HD] = tall_dot(scaled, pair_ref[...])
    give_ref[:, columns + 2 * HD :] = jnp.broadcast_to(square, (rows, HD))


def query_kernel(scaled_ref, own_ref, keep_ref):
    keep_ref[...] = tall_dot(scaled_ref[...], own_ref[...])


def attend_kernel(
    depth, step, ctx_ref, keep_ref, give_ref, got_ref, cos_ref, sin_ref, held_ref, fresh_ref, attended_ref,
    new_ref,
):
    rows, columns = attended_ref.shape
    chunks, parts = cos_ref.shape[0], new_ref.shape[1] // rows
    index = step - lax.axis_index("section")
    valid = jnp.logical_and(index >= 0, index < chunks)
    index = jnp.clip(index, 0, chunks - 1)
    batch, offset = index // parts, (index % parts) * rows
    length = ctx_ref[batch]
    cached = held_ref.shape[1]
    span = fresh_ref.shape[1]
    total = keep_ref[...] + got_ref[:, :columns]
    rest = give_ref[:, columns:] + got_ref[:, columns:]
    square = rest[:, 2 * HD : 2 * HD + 1]
    scale = lax.rsqrt(square / depth + EPS)
    cosine = cos_ref[index] * scale
    sine = sin_ref[index] * scale
    pair = rest[:, : 2 * HD]
    low = HD // 2
    keys = jnp.concatenate([pair[:, :low], pair[:, HD : HD + low]], axis=1)
    values = jnp.concatenate([pair[:, low:HD], pair[:, HD + low :]], axis=1) * scale
    new_ref[...] = fresh_ref[...]

    @pl.when(valid)
    def _():
        place = pl.ds(pl.multiple_of(offset, rows), rows)
        new_ref[batch, place, :HD] = turn(keys, cosine, sine).astype(jnp.bfloat16)
        new_ref[batch, place, HD:] = values.astype(jnp.bfloat16)

    live = lax.broadcasted_iota(jnp.int32, (1, cached), 1) < length
    row = lax.broadcasted_iota(jnp.int32, (rows, span), 0) + offset
    causal = lax.broadcasted_iota(jnp.int32, (rows, span), 1) <= row
    heads = columns // HD
    group = max(1, min(heads, 256 // rows))
    causal = jnp.concatenate([causal] * group, axis=0)
    root = math.log2(math.e) / math.sqrt(HD)
    cosine, sine = cosine * root, sine * root
    contract = (((1,), (1,)), ((), ()))
    for base in range(0, heads, group):
        queries = jnp.concatenate(
            [
                turn(total[:, h * HD : (h + 1) * HD], cosine, sine).astype(jnp.bfloat16)
                for h in range(base, base + group)
            ],
            axis=0,
        )
        scores = lax.dot_general(
            queries, held_ref[batch, :, :HD], contract, preferred_element_type=jnp.float32
        )
        scores = jnp.where(live, scores, -1e30)
        recent = lax.dot_general(
            queries, new_ref[batch, :, :HD], contract, preferred_element_type=jnp.float32
        )
        recent = jnp.where(causal, recent, -1e30)
        top = jnp.maximum(
            jnp.max(scores, axis=-1, keepdims=True), jnp.max(recent, axis=-1, keepdims=True)
        )
        scores = jnp.exp2(scores - top)
        recent = jnp.exp2(recent - top)
        weight = jnp.sum(scores, axis=-1, keepdims=True) + jnp.sum(recent, axis=-1, keepdims=True)
        mixed = dot(scores.astype(jnp.bfloat16), held_ref[batch, :, HD:]) + dot(
            recent.astype(jnp.bfloat16), new_ref[batch, :, HD:]
        )
        mixed = (mixed / weight).astype(jnp.bfloat16)
        for h in range(group):
            attended_ref[:, (base + h) * HD : (base + h + 1) * HD] = mixed[
                h * rows : (h + 1) * rows
            ]


def out_kernel(mine_ref, own_ref, part_ref):
    width = part_ref.shape[2]
    for j in range(part_ref.shape[0]):
        part_ref[j] = tall_dot(mine_ref[...], own_ref[:, j * width : (j + 1) * width])


def finish_kernel(part_ref, got_ref, other_ref, partial_ref):
    width = part_ref.shape[2]
    for j in range(part_ref.shape[0]):
        more = tall_dot(got_ref[...], other_ref[:, j * width : (j + 1) * width])
        partial_ref[j] = (part_ref[j] + more).astype(jnp.bfloat16)


def last_kernel(part_ref, got_ref, other_ref, fresh_ref, partial_ref):
    n_chip, rows, width = part_ref.shape
    micro, span, depth = fresh_ref.shape
    half = span // 2
    place = pl.ds(pl.multiple_of(lax.axis_index("core") * half, half), half)
    for j in range(n_chip):
        more = tall_dot(got_ref[...], other_ref[:, j * width : (j + 1) * width])
        partial_ref[j, :rows] = (part_ref[j] + more).astype(jnp.bfloat16)
        for m in range(micro):
            partial_ref[j, rows:, m * depth : (m + 1) * depth] = fresh_ref[m, place, :]


def enter_kernel(step, incoming_ref, inputs_ref, layer_ref, copies_ref):
    layer_ref[...] = incoming_ref[...]

    @pl.when(lax.axis_index("section") == 0)
    def _():
        layer_ref[...] = inputs_ref[step]

    for j in range(copies_ref.shape[0]):
        copies_ref[j] = layer_ref[...]


def settle_kernel(step, pieces_ref, layer_ref, done_ref, send_ref, new_ref):
    chunks = done_ref.shape[0]
    section = lax.axis_index("section")
    index = step - section
    total = layer_ref[...].astype(jnp.float32)
    rows = layer_ref.shape[0]
    summed = pieces_ref[0, :rows].astype(jnp.float32)
    for j in range(1, pieces_ref.shape[0]):
        summed += pieces_ref[j, :rows].astype(jnp.float32)
    updated = (total + summed).astype(jnp.bfloat16)
    send_ref[...] = updated
    new_ref[...] = done_ref[...]

    @pl.when(jnp.logical_and(index >= 0, index < chunks))
    def _():
        new_ref[jnp.clip(index, 0, chunks - 1)] = updated


def pick_kernel(holders_ref, blocks_ref, mine_ref, other_ref):
    heads, micro = holders_ref.shape
    count = heads * micro
    _, half, depth = mine_ref.shape
    below = blocks_ref.shape[1] - half
    holders = [holders_ref[e // micro, e % micro] for e in range(count)]
    core = lax.axis_index("core")
    first = 2 * lax.axis_index("chip")
    for ref, member in ((mine_ref, first + core), (other_ref, first + 1 - core)):
        ref[...] = jnp.zeros_like(ref)
        slot = jnp.int32(0)
        for e in range(count):
            here = holders[e] == member

            @pl.when(here)
            def _(slot=slot, e=e, ref=ref):
                ref[slot] = blocks_ref[
                    e // micro, below:, (e % micro) * depth : (e % micro + 1) * depth
                ]

            slot = jnp.minimum(slot + here.astype(jnp.int32), SLOTS - 1)


def move(copies, sems):
    started = [
        pltpu.make_async_copy(source, target, sems.at[i])
        for i, (source, target) in enumerate(copies)
    ]
    for copy in started:
        copy.start()
    for copy in started:
        copy.wait()


def strip(chip, core, width):
    return pl.ds(pl.multiple_of((2 * chip + core) * width, width), width)


def give_kernel(width, query_ref, pair_ref, cache_ref, out_ref, first_ref, second_ref, sems):
    other = 1 - lax.axis_index("core")
    columns = query_ref.shape[1]
    micro, length, depth = cache_ref.shape
    n_chip = query_ref.shape[0] // (2 * width)
    copies = []
    for j in range(n_chip):
        theirs, here = strip(j, other, width), pl.ds(j * width, width)
        copies.append((query_ref.at[theirs], first_ref.at[here, pl.ds(0, columns)]))
        copies.append((pair_ref.at[theirs], first_ref.at[here, pl.ds(columns, HD)]))
        copies.append((out_ref.at[:, theirs], second_ref.at[:, here]))
    for m in range(micro):
        place = first_ref.at[pl.ds(n_chip * width, length), pl.ds(m * depth, depth)]
        copies.append((cache_ref.at[m], place))
    move(copies, sems)


def keep_kernel(
    width, query_ref, pair_ref, cache_ref, out_ref, got_ref,
    own_query_ref, other_query_ref, both_ref, context_ref, own_out_ref, sems,
):
    core = lax.axis_index("core")
    columns = query_ref.shape[1]
    micro, length, depth = cache_ref.shape
    n_chip = query_ref.shape[0] // (2 * width)
    side = pl.ds(0, n_chip * width)
    own = pl.ds(pl.multiple_of(core * HD, HD), HD)
    other = pl.ds(pl.multiple_of((1 - core) * HD, HD), HD)
    early = pl.ds(pl.multiple_of(core * length, length), length)
    late = pl.ds(pl.multiple_of((1 - core) * length, length), length)
    copies = [
        (got_ref.at[side, pl.ds(0, columns)], other_query_ref),
        (got_ref.at[side, pl.ds(columns, HD)], both_ref.at[:, other]),
    ]
    for m in range(micro):
        got = got_ref.at[pl.ds(n_chip * width, length), pl.ds(m * depth, depth)]
        copies.append((got, context_ref.at[m, late]))
        copies.append((cache_ref.at[m], context_ref.at[m, early]))
    for j in range(n_chip):
        mine, here = strip(j, core, width), pl.ds(j * width, width)
        copies.append((query_ref.at[mine], own_query_ref.at[here]))
        copies.append((pair_ref.at[mine], both_ref.at[here, own]))
        copies.append((out_ref.at[:, mine], own_out_ref.at[:, here]))
    move(copies, sems)


def load_kernel(source_ref, target_ref, sems):
    move([(source_ref, target_ref)], sems)


def shuffle(kernel, out, inputs, copies):
    return pl.pallas_call(
        kernel,
        out_shape=out,
        in_specs=[pl.BlockSpec(memory_space=pl.ANY)] * inputs,
        out_specs=jax.tree.map(lambda _: pl.BlockSpec(memory_space=pl.ANY), out),
        scratch_shapes=[pltpu.SemaphoreType.DMA((copies,))],
        compiler_params=pltpu.CompilerParams(vmem_limit_bytes=2**20),
    )


def fast(x):
    return pltpu.with_memory_space_constraint(x, pltpu.VMEM)


def slow(x):
    return pltpu.with_memory_space_constraint(x, pltpu.HBM)


def call(kernel, out, flops, scalars, arrays, limit):
    return pl.pallas_call(
        kernel,
        out_shape=out,
        in_specs=[pl.BlockSpec(memory_space=pltpu.SMEM)] * scalars
        + [pl.BlockSpec(memory_space=pltpu.VMEM)] * arrays,
        out_specs=jax.tree.map(lambda _: pl.BlockSpec(memory_space=pltpu.VMEM), out),
        compiler_params=pltpu.CompilerParams(vmem_limit_bytes=limit * 2**20),
        cost_estimate=pl.CostEstimate(flops=flops, bytes_accessed=2**20, transcendentals=0),
    )


def shards(hidden_in, norm_gain, w_query, w_key_value, w_out, cache, ctx_len, placement):
    n_section = lax.axis_size("section")
    n_chip = lax.axis_size("chip")
    micro, span, width = hidden_in.shape
    rows = min(ROWS, span)
    parts = span // rows
    chunks = micro * parts
    steps = n_section + chunks - 1
    depth = n_chip * 2 * width
    side = depth // 2
    columns = w_query.shape[2]
    bf16, f32 = jnp.bfloat16, jnp.float32
    shape = jax.ShapeDtypeStruct

    def vmem(*dims):
        return pltpu.VMEM(dims, bf16)

    wq, wkv, wo, held = (slow(x[0]) for x in (w_query, w_key_value, w_out, cache))
    inputs = fast(hidden_in.reshape(chunks, rows, width))
    gain = fast(norm_gain)
    angle = shape((chunks, rows, HD), f32)
    state = shape((micro, span, 2 * HD), bf16)
    done_shape = shape((chunks, rows, width), bf16)
    packed = shape((rows, columns + 3 * HD), f32)
    block = shape((rows, columns), bf16)
    spread = shape((n_chip, rows, width), bf16)
    first, second = shuffle(
        functools.partial(give_kernel, width),
        (vmem(side + cache.shape[2], columns + HD), vmem(columns, side)),
        4,
        3 * n_chip + micro,
    )(wq, wkv, held, wo)
    first, second, ctx_len = lax.optimization_barrier((first, second, ctx_len))
    cosines, sines, fresh, done, layer_in, copies = call(
        functools.partial(table_kernel, parts),
        (angle, angle, state, done_shape, block, spread),
        2**20,
        1,
        1,
        4,
    )(ctx_len, inputs)
    got_first, got_second = swap(first), swap(second)
    features = exchange(copies)
    features, w_query, w_key_value, w_out, cache = lax.optimization_barrier(
        (features, w_query, w_key_value, w_out, cache)
    )
    wq, wkv, wo, held = (slow(x[0]) for x in (w_query, w_key_value, w_out, cache))
    wq_own, wq_other, w_pair, context, wo_own = shuffle(
        functools.partial(keep_kernel, width),
        (
            vmem(side, columns),
            vmem(side, columns),
            vmem(side, 2 * HD),
            vmem(micro, 2 * cache.shape[2], 2 * HD),
            vmem(columns, side),
        ),
        5,
        3 * n_chip + 2 + 2 * micro,
    )(wq, wkv, held, wo, got_first)
    wo_other = None
    wq_own, wo_own, w_pair, context, wq_other = (
        fast(v) for v in (wq_own, wo_own, w_pair, context, wq_other)
    )

    query_flops = rows * depth * columns
    project = call(
        project_kernel,
        (shape((rows, side), bf16), packed),
        query_flops + rows * depth * 2 * HD,
        0,
        4,
        4,
    )
    query = call(query_kernel, shape((rows, columns), f32), query_flops, 0, 2, 4)
    out = call(out_kernel, shape((n_chip, rows, width), f32), query_flops, 0, 2, 4)
    finish = call(finish_kernel, spread, query_flops, 0, 3, 4)
    last = call(
        last_kernel, shape((n_chip, rows + span // 2, width), bf16), query_flops, 0, 4, 4
    )
    for step in range(steps):
        if step > 0:
            if step < chunks:
                layer_in, copies = call(
                    functools.partial(enter_kernel, step),
                    (block, spread),
                    2**20,
                    0,
                    2,
                    4,
                )(layer_in, inputs)
            else:
                copies = jnp.broadcast_to(layer_in[None], (n_chip, rows, width))
            features = exchange(copies)
        scaled, give = project(features, gain, wq_other, w_pair)
        got = swap(give)
        keep = query(scaled, wq_own)
        attend = call(
            functools.partial(attend_kernel, depth, step),
            (block, state),
            4 * rows * columns * (context.shape[1] + span),
            1,
            7,
            12,
        )
        attended, fresh = attend(ctx_len, keep, give, got, cosines, sines, context, fresh)
        got = swap(attended)
        part = out(attended, wo_own)
        if step == 0:
            wo_other = fast(shuffle(load_kernel, vmem(columns, side), 1, 1)(got_second))
        if step + 1 < steps:
            pieces = exchange(finish(part, got, wo_other))
        else:
            pieces = exchange(last(part, got, wo_other, fresh))
        settle = call(
            functools.partial(settle_kernel, step), (block, done_shape), 2**20, 0, 3, 4
        )
        send, done = settle(pieces, layer_in, done)
        if step + 1 < steps:
            route = [
                (i, i + 1)
                for i in range(max(0, step - chunks + 1), min(step, n_section - 2) + 1)
            ]
            layer_in = lax.ppermute(send, "section", route)
    outputs = done.reshape(micro, span, width)

    slots = shape((SLOTS, span // 2, 2 * HD), bf16)
    mine, other = call(pick_kernel, (slots, slots), 2**20, 1, 1, 4)(placement[0], pieces)
    other = swap(other)
    store = jnp.where(
        lax.axis_index("core") == 0,
        jnp.concatenate([mine, other], axis=1),
        jnp.concatenate([other, mine], axis=1),
    )
    return (outputs[None], store[None])


def solution(mesh):
    n_section, n_tp = mesh.devices.shape
    fine = Mesh(mesh.devices.reshape(n_section, n_tp // 2, 2), ("section", "chip", "core"))
    tp = ("chip", "core")
    in_specs = (
        P(None, None, tp),
        P("section", None),
        P("section", None, tp),
        P("section", None, tp),
        P("section", tp, None),
        P("section", None, tp, None),
        P(),
        P("section", None, None),
    )
    out_specs = (P("section", None, None, tp), P("section", tp, None, None))
    return jax.shard_map(shards, mesh=fine, in_specs=in_specs, out_specs=out_specs, check_vma=False)
```

```python
import functools
import math

import jax
import jax.numpy as jnp
from jax import lax
from jax.experimental import pallas as pl
from jax.experimental.pallas import tpu as pltpu
from jax.sharding import Mesh
from jax.sharding import PartitionSpec as P

HD = 128
SLOTS = 2
EPS = 1e-05
ROWS = 64
TALL = 128


def swap(x):
    return lax.ppermute(x, "core", [(0, 1), (1, 0)])


def exchange(blocks):
    flat = blocks.reshape(blocks.shape[0] * blocks.shape[1], blocks.shape[2])
    moved = lax.all_to_all(flat, "chip", split_axis=0, concat_axis=0, tiled=True)
    return moved.reshape(blocks.shape)


def dot(a, b):
    return jnp.dot(a, b, preferred_element_type=jnp.float32)


def tall_dot(a, b):
    rows = a.shape[0]
    if rows >= TALL:
        return dot(a, b)
    return dot(jnp.concatenate([a, jnp.zeros((TALL - rows, a.shape[1]), a.dtype)], axis=0), b)[:rows]


def turn(values, cosine, sine):
    return values * cosine + pltpu.roll(values, HD // 2, 1) * sine


def project_kernel(x_ref, gain_ref, other_ref, pair_ref, scaled_ref, give_ref):
    n_chip, rows, width = x_ref.shape
    columns = other_ref.shape[1]
    core = lax.axis_index("core")
    square = jnp.zeros((rows, 1), jnp.float32)
    for j in range(n_chip):
        part = x_ref[j].astype(jnp.float32)
        square += jnp.sum(part * part, axis=-1, keepdims=True)
        scaled_ref[:, j * width : (j + 1) * width] = (
            part * gain_ref[:, strip(j, core, width)]
        ).astype(jnp.bfloat16)
    scaled = scaled_ref[...]
    give_ref[:, :columns] = tall_dot(scaled, other_ref[...])
    give_ref[:, columns : columns + 2 * HD] = tall_dot(scaled, pair_ref[...])
    give_ref[:, columns + 2 * HD :] = jnp.broadcast_to(square, (rows, HD))


def query_kernel(scaled_ref, own_ref, keep_ref):
    keep_ref[...] = tall_dot(scaled_ref[...], own_ref[...])


def attend_kernel(
    depth, step, ctx_ref, keep_ref, give_ref, got_ref, cos_ref, sin_ref, held_ref, fresh_ref, attended_ref,
    new_ref,
):
    rows, columns = attended_ref.shape
    chunks, parts = cos_ref.shape[0], new_ref.shape[1] // rows
    index = step - lax.axis_index("section")
    valid = jnp.logical_and(index >= 0, index < chunks)
    index = jnp.clip(index, 0, chunks - 1)
    batch, offset = index // parts, (index % parts) * rows
    length = ctx_ref[batch]
    cached = held_ref.shape[1]
    span = fresh_ref.shape[1]
    total = keep_ref[...] + got_ref[:, :columns]
    rest = give_ref[:, columns:] + got_ref[:, columns:]
    square = rest[:, 2 * HD : 2 * HD + 1]
    scale = lax.rsqrt(square / depth + EPS)
    cosine = cos_ref[index] * scale
    sine = sin_ref[index] * scale
    pair = rest[:, : 2 * HD]
    low = HD // 2
    keys = jnp.concatenate([pair[:, :low], pair[:, HD : HD + low]], axis=1)
    values = jnp.concatenate([pair[:, low:HD], pair[:, HD + low :]], axis=1) * scale
    new_ref[...] = fresh_ref[...]

    @pl.when(valid)
    def _():
        place = pl.ds(pl.multiple_of(offset, rows), rows)
        new_ref[batch, place, :HD] = turn(keys, cosine, sine).astype(jnp.bfloat16)
        new_ref[batch, place, HD:] = values.astype(jnp.bfloat16)

    live = lax.broadcasted_iota(jnp.int32, (1, cached), 1) < length
    row = lax.broadcasted_iota(jnp.int32, (rows, span), 0) + offset
    causal = lax.broadcasted_iota(jnp.int32, (rows, span), 1) <= row
    heads = columns // HD
    group = max(1, min(heads, 256 // rows))
    causal = jnp.concatenate([causal] * group, axis=0)
    root = math.log2(math.e) / math.sqrt(HD)
    cosine, sine = cosine * root, sine * root
    contract = (((1,), (1,)), ((), ()))
    piece = min(cached, 256)
    for base in range(0, heads, group):
        queries = jnp.concatenate(
            [
                turn(total[:, h * HD : (h + 1) * HD], cosine, sine).astype(jnp.bfloat16)
                for h in range(base, base + group)
            ],
            axis=0,
        )
        recent = lax.dot_general(
            queries, new_ref[batch, :, :HD], contract, preferred_element_type=jnp.float32
        )
        recent = jnp.where(causal, recent, -1e30)
        top = jnp.max(recent, axis=-1, keepdims=True)
        pieces = []
        for first in range(0, cached, piece):
            keys = held_ref[batch, first : first + piece, :HD]
            scores = lax.dot_general(queries, keys, contract, preferred_element_type=jnp.float32)
            scores = jnp.where(live[:, first : first + piece], scores, -1e30)
            top = jnp.maximum(top, jnp.max(scores, axis=-1, keepdims=True))
            pieces.append(scores)
        recent = jnp.exp2(recent - top)
        weight = jnp.sum(recent, axis=-1, keepdims=True)
        mixed = dot(recent.astype(jnp.bfloat16), new_ref[batch, :, HD:])
        for index, scores in enumerate(pieces):
            scores = jnp.exp2(scores - top)
            weight += jnp.sum(scores, axis=-1, keepdims=True)
            values = held_ref[batch, index * piece : (index + 1) * piece, HD:]
            mixed += dot(scores.astype(jnp.bfloat16), values)
        mixed = (mixed / weight).astype(jnp.bfloat16)
        for h in range(group):
            attended_ref[:, (base + h) * HD : (base + h + 1) * HD] = mixed[
                h * rows : (h + 1) * rows
            ]


def out_kernel(mine_ref, own_ref, part_ref):
    width = part_ref.shape[2]
    for j in range(part_ref.shape[0]):
        part_ref[j] = tall_dot(mine_ref[...], own_ref[:, j * width : (j + 1) * width])


def finish_kernel(part_ref, got_ref, other_ref, partial_ref):
    width = part_ref.shape[2]
    for j in range(part_ref.shape[0]):
        more = tall_dot(got_ref[...], other_ref[:, j * width : (j + 1) * width])
        partial_ref[j] = (part_ref[j] + more).astype(jnp.bfloat16)


def last_kernel(part_ref, got_ref, other_ref, fresh_ref, partial_ref):
    n_chip, rows, width = part_ref.shape
    micro, span, depth = fresh_ref.shape
    half = span // 2
    place = pl.ds(pl.multiple_of(lax.axis_index("core") * half, half), half)
    for j in range(n_chip):
        more = tall_dot(got_ref[...], other_ref[:, j * width : (j + 1) * width])
        partial_ref[j, :rows] = (part_ref[j] + more).astype(jnp.bfloat16)
        for m in range(micro):
            partial_ref[j, rows:, m * depth : (m + 1) * depth] = fresh_ref[m, place, :]


def enter_kernel(step, incoming_ref, inputs_ref, layer_ref, copies_ref):
    layer_ref[...] = incoming_ref[...]

    @pl.when(lax.axis_index("section") == 0)
    def _():
        layer_ref[...] = inputs_ref[step]

    for j in range(copies_ref.shape[0]):
        copies_ref[j] = layer_ref[...]


def settle_kernel(step, pieces_ref, layer_ref, done_ref, send_ref, new_ref):
    chunks = done_ref.shape[0]
    section = lax.axis_index("section")
    index = step - section
    total = layer_ref[...].astype(jnp.float32)
    rows = layer_ref.shape[0]
    summed = pieces_ref[0, :rows].astype(jnp.float32)
    for j in range(1, pieces_ref.shape[0]):
        summed += pieces_ref[j, :rows].astype(jnp.float32)
    updated = (total + summed).astype(jnp.bfloat16)
    send_ref[...] = updated
    new_ref[...] = done_ref[...]

    @pl.when(jnp.logical_and(index >= 0, index < chunks))
    def _():
        new_ref[jnp.clip(index, 0, chunks - 1)] = updated


def pick_kernel(holders_ref, blocks_ref, mine_ref, other_ref):
    heads, micro = holders_ref.shape
    count = heads * micro
    _, half, depth = mine_ref.shape
    below = blocks_ref.shape[1] - half
    holders = [holders_ref[e // micro, e % micro] for e in range(count)]
    core = lax.axis_index("core")
    first = 2 * lax.axis_index("chip")
    for ref, member in ((mine_ref, first + core), (other_ref, first + 1 - core)):
        ref[...] = jnp.zeros_like(ref)
        slot = jnp.int32(0)
        for e in range(count):
            here = holders[e] == member

            @pl.when(here)
            def _(slot=slot, e=e, ref=ref):
                ref[slot] = blocks_ref[
                    e // micro, below:, (e % micro) * depth : (e % micro + 1) * depth
                ]

            slot = jnp.minimum(slot + here.astype(jnp.int32), SLOTS - 1)


def begin(copies, sems):
    started = [
        pltpu.make_async_copy(source, target, sems.at[i])
        for i, (source, target) in enumerate(copies)
    ]
    for copy in started:
        copy.start()
    return started


def move(copies, sems):
    for copy in begin(copies, sems):
        copy.wait()


def strip(chip, core, width):
    return pl.ds(pl.multiple_of((2 * chip + core) * width, width), width)


def open_kernel(
    parts, width, ctx_ref, inputs_ref, query_ref, pair_ref, cache_ref, out_ref,
    cos_ref, sin_ref, fresh_ref, done_ref, layer_ref, copies_ref, first_ref, second_ref, sems,
):
    other = 1 - lax.axis_index("core")
    columns = query_ref.shape[1]
    micro, length, depth = cache_ref.shape
    n_chip = query_ref.shape[0] // (2 * width)
    copies = [(inputs_ref.at[0], layer_ref)]
    for j in range(n_chip):
        theirs, here = strip(j, other, width), pl.ds(j * width, width)
        copies.append((query_ref.at[theirs], first_ref.at[here, pl.ds(0, columns)]))
        copies.append((pair_ref.at[theirs], first_ref.at[here, pl.ds(columns, HD)]))
        copies.append((out_ref.at[:, theirs], second_ref.at[:, here]))
    for m in range(micro):
        place = first_ref.at[pl.ds(n_chip * width, length), pl.ds(m * depth, depth)]
        copies.append((cache_ref.at[m], place))
    started = begin(copies, sems)
    chunks, rows, _ = cos_ref.shape
    lane = lax.broadcasted_iota(jnp.int32, (1, HD), 1)
    upper = lane >= HD // 2
    index = jnp.where(upper, lane - HD // 2, lane).astype(jnp.float32)
    freqs = jnp.exp(index * (-2.0 * math.log(500000.0) / HD))
    row = lax.broadcasted_iota(jnp.int32, (rows, HD), 0)
    for c in range(chunks):
        positions = ctx_ref[c // parts] + (c % parts) * rows + row
        angles = positions.astype(jnp.float32) * freqs
        cos_ref[c] = jnp.cos(angles)
        sine = jnp.sin(angles)
        sin_ref[c] = jnp.where(upper, sine, -sine)
    fresh_ref[...] = jnp.zeros_like(fresh_ref)
    done_ref[...] = jnp.zeros_like(done_ref)
    started[0].wait()
    for j in range(n_chip):
        copies_ref[j] = layer_ref[...]
    for copy in started[1:]:
        copy.wait()


def first_kernel(
    width, x_ref, gain_ref, other_ref, pair_ref, query_ref, out_ref,
    scaled_ref, give_ref, own_query_ref, own_out_ref, sems,
):
    core = lax.axis_index("core")
    copies = []
    for j in range(x_ref.shape[0]):
        mine, here = strip(j, core, width), pl.ds(j * width, width)
        copies.append((query_ref.at[mine], own_query_ref.at[here]))
        copies.append((out_ref.at[:, mine], own_out_ref.at[:, here]))
    started = begin(copies, sems)
    project_kernel(x_ref, gain_ref, other_ref, pair_ref, scaled_ref, give_ref)
    for copy in started:
        copy.wait()


def keep_kernel(
    width, pair_ref, cache_ref, got_ref, other_query_ref, both_ref, context_ref, sems
):
    core = lax.axis_index("core")
    columns = other_query_ref.shape[1]
    micro, length, depth = cache_ref.shape
    n_chip = pair_ref.shape[0] // (2 * width)
    side = pl.ds(0, n_chip * width)
    own = pl.ds(pl.multiple_of(core * HD, HD), HD)
    other = pl.ds(pl.multiple_of((1 - core) * HD, HD), HD)
    early = pl.ds(pl.multiple_of(core * length, length), length)
    late = pl.ds(pl.multiple_of((1 - core) * length, length), length)
    copies = [
        (got_ref.at[side, pl.ds(0, columns)], other_query_ref),
        (got_ref.at[side, pl.ds(columns, HD)], both_ref.at[:, other]),
    ]
    for m in range(micro):
        got = got_ref.at[pl.ds(n_chip * width, length), pl.ds(m * depth, depth)]
        copies.append((got, context_ref.at[m, late]))
        copies.append((cache_ref.at[m], context_ref.at[m, early]))
    for j in range(n_chip):
        mine, here = strip(j, core, width), pl.ds(j * width, width)
        copies.append((pair_ref.at[mine], both_ref.at[here, own]))
    move(copies, sems)


def load_kernel(source_ref, target_ref, sems):
    move([(source_ref, target_ref)], sems)


def shuffle(kernel, out, inputs, copies):
    return pl.pallas_call(
        kernel,
        out_shape=out,
        in_specs=[pl.BlockSpec(memory_space=pl.ANY)] * inputs,
        out_specs=jax.tree.map(lambda _: pl.BlockSpec(memory_space=pl.ANY), out),
        scratch_shapes=[pltpu.SemaphoreType.DMA((copies,))],
        compiler_params=pltpu.CompilerParams(vmem_limit_bytes=2**20),
    )


def fast(x):
    return pltpu.with_memory_space_constraint(x, pltpu.VMEM)


def slow(x):
    return pltpu.with_memory_space_constraint(x, pltpu.HBM)


def call(kernel, out, flops, scalars, arrays, limit):
    return pl.pallas_call(
        kernel,
        out_shape=out,
        in_specs=[pl.BlockSpec(memory_space=pltpu.SMEM)] * scalars
        + [pl.BlockSpec(memory_space=pltpu.VMEM)] * arrays,
        out_specs=jax.tree.map(lambda _: pl.BlockSpec(memory_space=pltpu.VMEM), out),
        compiler_params=pltpu.CompilerParams(vmem_limit_bytes=limit * 2**20),
        cost_estimate=pl.CostEstimate(flops=flops, bytes_accessed=2**20, transcendentals=0),
    )


def shards(hidden_in, norm_gain, w_query, w_key_value, w_out, cache, ctx_len, placement):
    n_section = lax.axis_size("section")
    n_chip = lax.axis_size("chip")
    micro, span, width = hidden_in.shape
    rows = min(ROWS, span)
    parts = span // rows
    chunks = micro * parts
    steps = n_section + chunks - 1
    depth = n_chip * 2 * width
    side = depth // 2
    columns = w_query.shape[2]
    bf16, f32 = jnp.bfloat16, jnp.float32
    shape = jax.ShapeDtypeStruct

    def vmem(*dims):
        return pltpu.VMEM(dims, bf16)

    wq, wkv, wo, held = (slow(x[0]) for x in (w_query, w_key_value, w_out, cache))
    inputs = fast(hidden_in.reshape(chunks, rows, width))
    gain = fast(norm_gain)
    angle = shape((chunks, rows, HD), f32)
    state = shape((micro, span, 2 * HD), bf16)
    done_shape = shape((chunks, rows, width), bf16)
    packed = shape((rows, columns + 3 * HD), f32)
    block = shape((rows, columns), bf16)
    spread = shape((n_chip, rows, width), bf16)
    anywhere, inside = pl.BlockSpec(memory_space=pl.ANY), pl.BlockSpec(memory_space=pltpu.VMEM)
    cosines, sines, fresh, done, layer_in, copies, first, second = pl.pallas_call(
        functools.partial(open_kernel, parts, width),
        out_shape=(
            angle,
            angle,
            state,
            done_shape,
            block,
            spread,
            vmem(side + cache.shape[2], columns + HD),
            vmem(columns, side),
        ),
        in_specs=[pl.BlockSpec(memory_space=pltpu.SMEM)] + [anywhere] * 5,
        out_specs=(inside,) * 6 + (anywhere,) * 2,
        scratch_shapes=[pltpu.SemaphoreType.DMA((3 * n_chip + micro + 1,))],
        compiler_params=pltpu.CompilerParams(vmem_limit_bytes=4 * 2**20),
    )(ctx_len, slow(hidden_in.reshape(chunks, rows, width)), wq, wkv, held, wo)
    got_first, got_second = swap(first), swap(second)
    features = exchange(copies)
    wq, wo = fast(w_query[0]), fast(w_out[0])
    features, w_key_value, cache = lax.optimization_barrier((features, w_key_value, cache))
    wkv, held = slow(w_key_value[0]), slow(cache[0])
    wq_other, w_pair, context = shuffle(
        functools.partial(keep_kernel, width),
        (
            vmem(side, columns),
            vmem(side, 2 * HD),
            vmem(micro, 2 * cache.shape[2], 2 * HD),
        ),
        3,
        n_chip + 2 + 2 * micro,
    )(wkv, held, got_first)
    w_pair, context, wq_other = (fast(v) for v in (w_pair, context, wq_other))

    query_flops = rows * depth * columns
    project = call(
        project_kernel,
        (shape((rows, side), bf16), packed),
        query_flops + rows * depth * 2 * HD,
        0,
        4,
        4,
    )
    query = call(query_kernel, shape((rows, columns), f32), query_flops, 0, 2, 4)
    out = call(out_kernel, shape((n_chip, rows, width), f32), query_flops, 0, 2, 4)
    finish = call(finish_kernel, spread, query_flops, 0, 3, 4)
    last = call(
        last_kernel, shape((n_chip, rows + span // 2, width), bf16), query_flops, 0, 4, 4
    )
    for step in range(steps):
        if step > 0:
            if step < chunks:
                layer_in, copies = call(
                    functools.partial(enter_kernel, step),
                    (block, spread),
                    2**20,
                    0,
                    2,
                    4,
                )(layer_in, inputs)
            else:
                copies = jnp.broadcast_to(layer_in[None], (n_chip, rows, width))
            features = exchange(copies)
        if step > 0:
            scaled, give = project(features, gain, wq_other, w_pair)
        else:
            scaled, give, wq_own, wo_own = pl.pallas_call(
                functools.partial(first_kernel, width),
                out_shape=(
                    shape((rows, side), bf16),
                    packed,
                    vmem(side, columns),
                    vmem(columns, side),
                ),
                in_specs=[inside] * 4 + [anywhere] * 2,
                out_specs=(inside,) * 2 + (anywhere,) * 2,
                scratch_shapes=[pltpu.SemaphoreType.DMA((2 * n_chip,))],
                compiler_params=pltpu.CompilerParams(vmem_limit_bytes=4 * 2**20),
            )(features, gain, wq_other, w_pair, wq, wo)
            wq_own, wo_own = fast(wq_own), fast(wo_own)
        got = swap(give)
        keep = query(scaled, wq_own)
        attend = call(
            functools.partial(attend_kernel, depth, step),
            (block, state),
            4 * rows * columns * (context.shape[1] + span),
            1,
            7,
            12,
        )
        attended, fresh = attend(ctx_len, keep, give, got, cosines, sines, context, fresh)
        got = swap(attended)
        part = out(attended, wo_own)
        if step == 0:
            wo_other = fast(shuffle(load_kernel, vmem(columns, side), 1, 1)(got_second))
        if step + 1 < steps:
            pieces = exchange(finish(part, got, wo_other))
        else:
            pieces = exchange(last(part, got, wo_other, fresh))
        settle = call(
            functools.partial(settle_kernel, step), (block, done_shape), 2**20, 0, 3, 4
        )
        send, done = settle(pieces, layer_in, done)
        if step + 1 < steps:
            route = [
                (i, i + 1)
                for i in range(max(0, step - chunks + 1), min(step, n_section - 2) + 1)
            ]
            layer_in = lax.ppermute(send, "section", route)
    outputs = done.reshape(micro, span, width)

    slots = shape((SLOTS, span // 2, 2 * HD), bf16)
    mine, other = call(pick_kernel, (slots, slots), 2**20, 1, 1, 4)(placement[0], pieces)
    other = swap(other)
    store = jnp.where(
        lax.axis_index("core") == 0,
        jnp.concatenate([mine, other], axis=1),
        jnp.concatenate([other, mine], axis=1),
    )
    return (outputs[None], store[None])


def solution(mesh):
    n_section, n_tp = mesh.devices.shape
    fine = Mesh(mesh.devices.reshape(n_section, n_tp // 2, 2), ("section", "chip", "core"))
    tp = ("chip", "core")
    in_specs = (
        P(None, None, tp),
        P("section", None),
        P("section", None, tp),
        P("section", None, tp),
        P("section", tp, None),
        P("section", None, tp, None),
        P(),
        P("section", None, None),
    )
    out_specs = (P("section", None, None, tp), P("section", tp, None, None))
    return jax.shard_map(shards, mesh=fine, in_specs=in_specs, out_specs=out_specs, check_vma=False)
```

```python
import functools
import math

import jax
import jax.numpy as jnp
from jax import lax
from jax.experimental import pallas as pl
from jax.experimental.pallas import tpu as pltpu
from jax.sharding import Mesh
from jax.sharding import PartitionSpec as P

HD = 128
SLOTS = 2
EPS = 1e-05
ROWS = 64
TALL = 128


def swap(x):
    return lax.ppermute(x, "core", [(0, 1), (1, 0)])


def exchange(blocks):
    flat = blocks.reshape(blocks.shape[0] * blocks.shape[1], blocks.shape[2])
    moved = lax.all_to_all(flat, "chip", split_axis=0, concat_axis=0, tiled=True)
    return moved.reshape(blocks.shape)


def dot(a, b):
    return jnp.dot(a, b, preferred_element_type=jnp.float32)


def tall_dot(a, b):
    rows = a.shape[0]
    if rows >= TALL:
        return dot(a, b)
    return dot(jnp.concatenate([a, jnp.zeros((TALL - rows, a.shape[1]), a.dtype)], axis=0), b)[:rows]


def turn(values, cosine, sine):
    return values * cosine + pltpu.roll(values, HD // 2, 1) * sine


def project_kernel(x_ref, gain_ref, other_ref, pair_ref, scaled_ref, give_ref):
    n_chip, rows, width = x_ref.shape
    columns = other_ref.shape[1]
    core = lax.axis_index("core")
    square = jnp.zeros((rows, 1), jnp.float32)
    for j in range(n_chip):
        part = x_ref[j].astype(jnp.float32)
        square += jnp.sum(part * part, axis=-1, keepdims=True)
        scaled_ref[:, j * width : (j + 1) * width] = (
            part * gain_ref[:, strip(j, core, width)]
        ).astype(jnp.bfloat16)
    scaled = scaled_ref[...]
    give_ref[:, :columns] = tall_dot(scaled, other_ref[...])
    give_ref[:, columns : columns + 2 * HD] = tall_dot(scaled, pair_ref[...])
    give_ref[:, columns + 2 * HD :] = jnp.broadcast_to(square, (rows, HD))


def query_kernel(scaled_ref, own_ref, keep_ref):
    keep_ref[...] = tall_dot(scaled_ref[...], own_ref[...])


def attend_kernel(
    depth, step, ctx_ref, keep_ref, give_ref, got_ref, cos_ref, sin_ref, held_ref, fresh_ref, attended_ref,
    new_ref,
):
    rows, columns = attended_ref.shape
    chunks, parts = cos_ref.shape[0], new_ref.shape[1] // rows
    index = step - lax.axis_index("section")
    valid = jnp.logical_and(index >= 0, index < chunks)
    index = jnp.clip(index, 0, chunks - 1)
    batch, offset = index // parts, (index % parts) * rows
    length = ctx_ref[batch]
    cached = held_ref.shape[1]
    span = fresh_ref.shape[1]
    total = keep_ref[...] + got_ref[:, :columns]
    rest = give_ref[:, columns:] + got_ref[:, columns:]
    square = rest[:, 2 * HD : 2 * HD + 1]
    scale = lax.rsqrt(square / depth + EPS)
    cosine = cos_ref[index] * scale
    sine = sin_ref[index] * scale
    pair = rest[:, : 2 * HD]
    low = HD // 2
    keys = jnp.concatenate([pair[:, :low], pair[:, HD : HD + low]], axis=1)
    values = jnp.concatenate([pair[:, low:HD], pair[:, HD + low :]], axis=1) * scale
    new_ref[...] = fresh_ref[...]

    @pl.when(valid)
    def _():
        place = pl.ds(pl.multiple_of(offset, rows), rows)
        new_ref[batch, place, :HD] = turn(keys, cosine, sine).astype(jnp.bfloat16)
        new_ref[batch, place, HD:] = values.astype(jnp.bfloat16)

    live = lax.broadcasted_iota(jnp.int32, (1, cached), 1) < length
    row = lax.broadcasted_iota(jnp.int32, (rows, span), 0) + offset
    causal = lax.broadcasted_iota(jnp.int32, (rows, span), 1) <= row
    heads = columns // HD
    group = max(1, min(heads, 256 // rows))
    causal = jnp.concatenate([causal] * group, axis=0)
    root = math.log2(math.e) / math.sqrt(HD)
    cosine, sine = cosine * root, sine * root
    contract = (((1,), (1,)), ((), ()))
    piece = min(cached, 256)
    for base in range(0, heads, group):
        queries = jnp.concatenate(
            [
                turn(total[:, h * HD : (h + 1) * HD], cosine, sine).astype(jnp.bfloat16)
                for h in range(base, base + group)
            ],
            axis=0,
        )
        recent = lax.dot_general(
            queries, new_ref[batch, :, :HD], contract, preferred_element_type=jnp.float32
        )
        recent = jnp.where(causal, recent, -1e30)
        top = jnp.max(recent, axis=-1, keepdims=True)
        pieces = []
        for first in range(0, cached, piece):
            keys = held_ref[batch, first : first + piece, :HD]
            scores = lax.dot_general(queries, keys, contract, preferred_element_type=jnp.float32)
            scores = jnp.where(live[:, first : first + piece], scores, -1e30)
            top = jnp.maximum(top, jnp.max(scores, axis=-1, keepdims=True))
            pieces.append(scores)
        recent = jnp.exp2(recent - top)
        weight = jnp.sum(recent, axis=-1, keepdims=True)
        mixed = dot(recent.astype(jnp.bfloat16), new_ref[batch, :, HD:])
        for index, scores in enumerate(pieces):
            scores = jnp.exp2(scores - top)
            weight += jnp.sum(scores, axis=-1, keepdims=True)
            values = held_ref[batch, index * piece : (index + 1) * piece, HD:]
            mixed += dot(scores.astype(jnp.bfloat16), values)
        mixed = (mixed / weight).astype(jnp.bfloat16)
        for h in range(group):
            attended_ref[:, (base + h) * HD : (base + h + 1) * HD] = mixed[
                h * rows : (h + 1) * rows
            ]


def out_kernel(mine_ref, own_ref, part_ref):
    width = part_ref.shape[2]
    for j in range(part_ref.shape[0]):
        part_ref[j] = tall_dot(mine_ref[...], own_ref[:, j * width : (j + 1) * width])


def finish_kernel(part_ref, got_ref, other_ref, partial_ref):
    width = part_ref.shape[2]
    for j in range(part_ref.shape[0]):
        more = tall_dot(got_ref[...], other_ref[:, j * width : (j + 1) * width])
        partial_ref[j] = (part_ref[j] + more).astype(jnp.bfloat16)


def last_kernel(part_ref, got_ref, other_ref, fresh_ref, partial_ref):
    n_chip, rows, width = part_ref.shape
    micro, span, depth = fresh_ref.shape
    half = span // 2
    place = pl.ds(pl.multiple_of(lax.axis_index("core") * half, half), half)
    for j in range(n_chip):
        more = tall_dot(got_ref[...], other_ref[:, j * width : (j + 1) * width])
        partial_ref[j, :rows] = (part_ref[j] + more).astype(jnp.bfloat16)
        for m in range(micro):
            partial_ref[j, rows:, m * depth : (m + 1) * depth] = fresh_ref[m, place, :]


def enter_kernel(step, incoming_ref, inputs_ref, layer_ref, copies_ref):
    layer_ref[...] = incoming_ref[...]

    @pl.when(lax.axis_index("section") == 0)
    def _():
        layer_ref[...] = inputs_ref[step]

    for j in range(copies_ref.shape[0]):
        copies_ref[j] = layer_ref[...]


def settle_kernel(step, pieces_ref, layer_ref, done_ref, send_ref, new_ref):
    chunks = done_ref.shape[0]
    section = lax.axis_index("section")
    index = step - section
    total = layer_ref[...].astype(jnp.float32)
    rows = layer_ref.shape[0]
    summed = pieces_ref[0, :rows].astype(jnp.float32)
    for j in range(1, pieces_ref.shape[0]):
        summed += pieces_ref[j, :rows].astype(jnp.float32)
    updated = (total + summed).astype(jnp.bfloat16)
    send_ref[...] = updated
    new_ref[...] = done_ref[...]

    @pl.when(jnp.logical_and(index >= 0, index < chunks))
    def _():
        new_ref[jnp.clip(index, 0, chunks - 1)] = updated


def pick_kernel(holders_ref, blocks_ref, mine_ref, other_ref):
    heads, micro = holders_ref.shape
    count = heads * micro
    _, half, depth = mine_ref.shape
    below = blocks_ref.shape[1] - half
    holders = [holders_ref[e // micro, e % micro] for e in range(count)]
    core = lax.axis_index("core")
    first = 2 * lax.axis_index("chip")
    for ref, member in ((mine_ref, first + core), (other_ref, first + 1 - core)):
        ref[...] = jnp.zeros_like(ref)
        slot = jnp.int32(0)
        for e in range(count):
            here = holders[e] == member

            @pl.when(here)
            def _(slot=slot, e=e, ref=ref):
                ref[slot] = blocks_ref[
                    e // micro, below:, (e % micro) * depth : (e % micro + 1) * depth
                ]

            slot = jnp.minimum(slot + here.astype(jnp.int32), SLOTS - 1)


def begin(copies, sems):
    started = [
        pltpu.make_async_copy(source, target, sems.at[i])
        for i, (source, target) in enumerate(copies)
    ]
    for copy in started:
        copy.start()
    return started


def move(copies, sems):
    for copy in begin(copies, sems):
        copy.wait()


def strip(chip, core, width):
    return pl.ds(pl.multiple_of((2 * chip + core) * width, width), width)


def open_kernel(
    parts, width, ctx_ref, inputs_ref, query_ref, pair_ref, cache_ref, out_ref,
    cos_ref, sin_ref, fresh_ref, done_ref, layer_ref, copies_ref, first_ref, second_ref, sems,
):
    other = 1 - lax.axis_index("core")
    columns = query_ref.shape[1]
    micro, length, depth = cache_ref.shape
    n_chip = query_ref.shape[0] // (2 * width)
    copies = [(inputs_ref.at[0], layer_ref)]
    for j in range(n_chip):
        theirs, here = strip(j, other, width), pl.ds(j * width, width)
        copies.append((query_ref.at[theirs], first_ref.at[here, pl.ds(0, columns)]))
        copies.append((pair_ref.at[theirs], first_ref.at[here, pl.ds(columns, HD)]))
        copies.append((out_ref.at[:, theirs], second_ref.at[:, here]))
    for m in range(micro):
        place = first_ref.at[pl.ds(n_chip * width, length), pl.ds(m * depth, depth)]
        copies.append((cache_ref.at[m], place))
    started = begin(copies, sems)
    chunks, rows, _ = cos_ref.shape
    lane = lax.broadcasted_iota(jnp.int32, (1, HD), 1)
    upper = lane >= HD // 2
    index = jnp.where(upper, lane - HD // 2, lane).astype(jnp.float32)
    freqs = jnp.exp(index * (-2.0 * math.log(500000.0) / HD))
    row = lax.broadcasted_iota(jnp.int32, (rows, HD), 0)
    for c in range(chunks):
        positions = ctx_ref[c // parts] + (c % parts) * rows + row
        angles = positions.astype(jnp.float32) * freqs
        cos_ref[c] = jnp.cos(angles)
        sine = jnp.sin(angles)
        sin_ref[c] = jnp.where(upper, sine, -sine)
    fresh_ref[...] = jnp.zeros_like(fresh_ref)
    done_ref[...] = jnp.zeros_like(done_ref)
    started[0].wait()
    for j in range(n_chip):
        copies_ref[j] = layer_ref[...]
    for copy in started[1:]:
        copy.wait()


def first_kernel(
    width, x_ref, gain_ref, other_ref, pair_ref, query_ref, out_ref,
    scaled_ref, give_ref, own_query_ref, own_out_ref, sems,
):
    core = lax.axis_index("core")
    copies = []
    for j in range(x_ref.shape[0]):
        mine, here = strip(j, core, width), pl.ds(j * width, width)
        copies.append((query_ref.at[mine], own_query_ref.at[here]))
        copies.append((out_ref.at[:, mine], own_out_ref.at[:, here]))
    started = begin(copies, sems)
    project_kernel(x_ref, gain_ref, other_ref, pair_ref, scaled_ref, give_ref)
    for copy in started:
        copy.wait()


def keep_kernel(
    width, pair_ref, cache_ref, got_ref, other_query_ref, both_ref, context_ref, sems
):
    core = lax.axis_index("core")
    columns = other_query_ref.shape[1]
    micro, length, depth = cache_ref.shape
    n_chip = pair_ref.shape[0] // (2 * width)
    side = pl.ds(0, n_chip * width)
    own = pl.ds(pl.multiple_of(core * HD, HD), HD)
    other = pl.ds(pl.multiple_of((1 - core) * HD, HD), HD)
    early = pl.ds(pl.multiple_of(core * length, length), length)
    late = pl.ds(pl.multiple_of((1 - core) * length, length), length)
    copies = [
        (got_ref.at[side, pl.ds(0, columns)], other_query_ref),
        (got_ref.at[side, pl.ds(columns, HD)], both_ref.at[:, other]),
    ]
    for m in range(micro):
        got = got_ref.at[pl.ds(n_chip * width, length), pl.ds(m * depth, depth)]
        copies.append((got, context_ref.at[m, late]))
        copies.append((cache_ref.at[m], context_ref.at[m, early]))
    for j in range(n_chip):
        mine, here = strip(j, core, width), pl.ds(j * width, width)
        copies.append((pair_ref.at[mine], both_ref.at[here, own]))
    move(copies, sems)


def load_kernel(source_ref, target_ref, sems):
    move([(source_ref, target_ref)], sems)


def shuffle(kernel, out, inputs, copies):
    return pl.pallas_call(
        kernel,
        out_shape=out,
        in_specs=[pl.BlockSpec(memory_space=pl.ANY)] * inputs,
        out_specs=jax.tree.map(lambda _: pl.BlockSpec(memory_space=pl.ANY), out),
        scratch_shapes=[pltpu.SemaphoreType.DMA((copies,))],
        compiler_params=pltpu.CompilerParams(vmem_limit_bytes=2**20),
    )


def fast(x):
    return pltpu.with_memory_space_constraint(x, pltpu.VMEM)


def slow(x):
    return pltpu.with_memory_space_constraint(x, pltpu.HBM)


def call(kernel, out, flops, scalars, arrays, limit):
    return pl.pallas_call(
        kernel,
        out_shape=out,
        in_specs=[pl.BlockSpec(memory_space=pltpu.SMEM)] * scalars
        + [pl.BlockSpec(memory_space=pltpu.VMEM)] * arrays,
        out_specs=jax.tree.map(lambda _: pl.BlockSpec(memory_space=pltpu.VMEM), out),
        compiler_params=pltpu.CompilerParams(vmem_limit_bytes=limit * 2**20),
        cost_estimate=pl.CostEstimate(flops=flops, bytes_accessed=2**20, transcendentals=0),
    )


def shards(hidden_in, norm_gain, w_query, w_key_value, w_out, cache, ctx_len, placement):
    n_section = lax.axis_size("section")
    n_chip = lax.axis_size("chip")
    micro, span, width = hidden_in.shape
    rows = min(ROWS, span)
    parts = span // rows
    chunks = micro * parts
    steps = n_section + chunks - 1
    depth = n_chip * 2 * width
    side = depth // 2
    columns = w_query.shape[2]
    bf16, f32 = jnp.bfloat16, jnp.float32
    shape = jax.ShapeDtypeStruct

    def vmem(*dims):
        return pltpu.VMEM(dims, bf16)

    wq, wkv, wo, held = (slow(x[0]) for x in (w_query, w_key_value, w_out, cache))
    inputs = fast(hidden_in.reshape(chunks, rows, width))
    angle = shape((chunks, rows, HD), f32)
    state = shape((micro, span, 2 * HD), bf16)
    done_shape = shape((chunks, rows, width), bf16)
    packed = shape((rows, columns + 3 * HD), f32)
    block = shape((rows, columns), bf16)
    spread = shape((n_chip, rows, width), bf16)
    anywhere, inside = pl.BlockSpec(memory_space=pl.ANY), pl.BlockSpec(memory_space=pltpu.VMEM)
    cosines, sines, fresh, done, layer_in, copies, first, second = pl.pallas_call(
        functools.partial(open_kernel, parts, width),
        out_shape=(
            angle,
            angle,
            state,
            done_shape,
            block,
            spread,
            vmem(side + cache.shape[2], columns + HD),
            vmem(columns, side),
        ),
        in_specs=[pl.BlockSpec(memory_space=pltpu.SMEM)] + [anywhere] * 5,
        out_specs=(inside,) * 6 + (anywhere,) * 2,
        scratch_shapes=[pltpu.SemaphoreType.DMA((3 * n_chip + micro + 1,))],
        compiler_params=pltpu.CompilerParams(vmem_limit_bytes=4 * 2**20),
    )(ctx_len, slow(hidden_in.reshape(chunks, rows, width)), wq, wkv, held, wo)
    first, norm_gain = lax.optimization_barrier((first, norm_gain))
    gain = fast(norm_gain)
    got_first, got_second = swap(first), swap(second)
    features = exchange(copies)
    wq, wo = fast(w_query[0]), slow(w_out[0])
    features, w_key_value, cache = lax.optimization_barrier((features, w_key_value, cache))
    wkv, held = slow(w_key_value[0]), slow(cache[0])
    wq_other, w_pair, context = shuffle(
        functools.partial(keep_kernel, width),
        (
            vmem(side, columns),
            vmem(side, 2 * HD),
            vmem(micro, 2 * cache.shape[2], 2 * HD),
        ),
        3,
        n_chip + 2 + 2 * micro,
    )(wkv, held, got_first)
    w_pair, context, wq_other = (fast(v) for v in (w_pair, context, wq_other))

    query_flops = rows * depth * columns
    project = call(
        project_kernel,
        (shape((rows, side), bf16), packed),
        query_flops + rows * depth * 2 * HD,
        0,
        4,
        4,
    )
    query = call(query_kernel, shape((rows, columns), f32), query_flops, 0, 2, 4)
    out = call(out_kernel, shape((n_chip, rows, width), f32), query_flops, 0, 2, 4)
    finish = call(finish_kernel, spread, query_flops, 0, 3, 4)
    last = call(
        last_kernel, shape((n_chip, rows + span // 2, width), bf16), query_flops, 0, 4, 4
    )
    for step in range(steps):
        if step > 0:
            if step < chunks:
                layer_in, copies = call(
                    functools.partial(enter_kernel, step),
                    (block, spread),
                    2**20,
                    0,
                    2,
                    4,
                )(layer_in, inputs)
            else:
                copies = jnp.broadcast_to(layer_in[None], (n_chip, rows, width))
            features = exchange(copies)
        if step > 0:
            scaled, give = project(features, gain, wq_other, w_pair)
        else:
            scaled, give, wq_own, wo_own = pl.pallas_call(
                functools.partial(first_kernel, width),
                out_shape=(
                    shape((rows, side), bf16),
                    packed,
                    vmem(side, columns),
                    vmem(columns, side),
                ),
                in_specs=[inside] * 4 + [anywhere] * 2,
                out_specs=(inside,) * 2 + (anywhere,) * 2,
                scratch_shapes=[pltpu.SemaphoreType.DMA((2 * n_chip,))],
                compiler_params=pltpu.CompilerParams(vmem_limit_bytes=4 * 2**20),
            )(features, gain, wq_other, w_pair, wq, wo)
            wq_own, wo_own = fast(wq_own), fast(wo_own)
        got = swap(give)
        keep = query(scaled, wq_own)
        attend = call(
            functools.partial(attend_kernel, depth, step),
            (block, state),
            4 * rows * columns * (context.shape[1] + span),
            1,
            7,
            12,
        )
        attended, fresh = attend(ctx_len, keep, give, got, cosines, sines, context, fresh)
        got = swap(attended)
        part = out(attended, wo_own)
        if step == 0:
            wo_other = fast(shuffle(load_kernel, vmem(columns, side), 1, 1)(got_second))
        if step + 1 < steps:
            pieces = exchange(finish(part, got, wo_other))
        else:
            pieces = exchange(last(part, got, wo_other, fresh))
        settle = call(
            functools.partial(settle_kernel, step), (block, done_shape), 2**20, 0, 3, 4
        )
        send, done = settle(pieces, layer_in, done)
        if step + 1 < steps:
            route = [
                (i, i + 1)
                for i in range(max(0, step - chunks + 1), min(step, n_section - 2) + 1)
            ]
            layer_in = lax.ppermute(send, "section", route)
    outputs = done.reshape(micro, span, width)

    slots = shape((SLOTS, span // 2, 2 * HD), bf16)
    mine, other = call(pick_kernel, (slots, slots), 2**20, 1, 1, 4)(placement[0], pieces)
    other = swap(other)
    store = jnp.where(
        lax.axis_index("core") == 0,
        jnp.concatenate([mine, other], axis=1),
        jnp.concatenate([other, mine], axis=1),
    )
    return (outputs[None], store[None])


def solution(mesh):
    n_section, n_tp = mesh.devices.shape
    fine = Mesh(mesh.devices.reshape(n_section, n_tp // 2, 2), ("section", "chip", "core"))
    tp = ("chip", "core")
    in_specs = (
        P(None, None, tp),
        P("section", None),
        P("section", None, tp),
        P("section", None, tp),
        P("section", tp, None),
        P("section", None, tp, None),
        P(),
        P("section", None, None),
    )
    out_specs = (P("section", None, None, tp), P("section", tp, None, None))
    return jax.shard_map(shards, mesh=fine, in_specs=in_specs, out_specs=out_specs, check_vma=False)
```
